256 devices in a mesh: region: 32 (over x, z_lo, y), tm: 8 (over z_hi, core).
Axes of the slice: x: 4, y: 4, z: 8 (z_hi: 4, z_lo: 2; z = z_hi * 2 + z_lo), core: 2. Of those that a mesh axis runs over, the one named last changes fastest.
Arguments:
- latents: bfloat16 [32, 1024, 768], P('region', 'tm')
- output_grad: bfloat16 [32, 1024, 768], P('region', 'tm'), may hold values from -6 to 6
- conv_kernel: float32 [4, 768], replicated, may hold values from -1 to 1
- w_query: bfloat16 [768, 768], replicated, may hold values from -0.21875 to 0.21875
- w_key: bfloat16 [768, 768], replicated, may hold values from -0.21875 to 0.21875
- w_value: bfloat16 [768, 768], replicated, may hold values from -0.21875 to 0.21875
- w_out: bfloat16 [768, 768], replicated, may hold values from -0.21875 to 0.21875
- live_counts: int32 [32, 8], P('region', 'tm'), may hold values from 1 to 128, as said below
Outputs:
- input_grad: bfloat16 [32, 1024, 768], P('region', 'tm')
The draws below stay inside these ranges and needn't reach their ends.
Inputs may be any that keep to these rules, and one draw needn't show every extreme that they name: The first live_counts[r, c] of the 128 tokens of region r in span c are valid.
All inputs are finite; a program needn't handle non-finite values.
Results may differ from the reference program's by a relative error of at most 0.018.
The reference program's roundings to bfloat16 on the way (of `hidden`, `grad_proj`, `score_grad` and `query_grad`) count: a program that leaves them out, or rounds other values in their place, can miss the bound.
Values may be sent and summed in bfloat16 or wider, within the bound.
No kernel may reach another device: no remote copies, remote signals or barrier semaphores. Data moves between devices by JAX's collectives and lax.ppermute only.
A program may use at most 128 MiB of HBM per device.

```python
import math
import jax
import jax.numpy as jnp
from jax import lax

D = 768
H = 12
HD = 64
KW = 4
TCH = 128
REGIONS = 32
TIME = 1024
N_REGION = 32
N_TM = 8


def draw_latents(key, part):
    base = jax.random.normal(key, (REGIONS, TIME, D), jnp.float32)
    return base.astype(jnp.bfloat16)


def draw_live_counts(key, part):
    first = jax.random.randint(jax.random.fold_in(key, 11), (REGIONS, N_TM), 1, TCH + 1)
    second = jax.random.randint(jax.random.fold_in(key, 12), (REGIONS, N_TM), 1, TCH + 1)
    counts = jnp.minimum(first, second)
    counts = counts.at[0].set(TCH)
    return counts.astype(jnp.int32)


def steps_of(stream_key, dims, cuts, least, high):
    gain = 1.0
    for dim, shards_of in cuts:
        steps = jax.random.uniform(jax.random.fold_in(jax.random.fold_in(stream_key, 6), dim), (shards_of,), jnp.float32, least / len(cuts), high / len(cuts))
        gain = gain * jnp.repeat(jnp.exp(steps), dims[dim] // shards_of).reshape((-1,) + (1,) * (len(dims) - 1 - dim))
    return gain


def scatter_about(key, extent, spread, bound, pieces=(), kind=jnp.bfloat16):
    values = spread * jax.random.normal(key, extent, jnp.float32)
    if pieces:
        values = values * steps_of(key, extent, pieces, -0.22, 0.18)
    return jnp.clip(values, -bound, bound).astype(kind)


def setup_inputs(seed: int = 0) -> dict:
    splits = jax.random.split(jax.random.key(seed), 9)
    return {
        "latents": draw_latents(jax.random.fold_in(splits[8], 71), 0),
        "output_grad": scatter_about(splits[1], (REGIONS, TIME, D), 1.0, 6.0, ((0, 32), (1, 8))),
        "conv_kernel": jnp.clip(jax.random.uniform(splits[2], (KW, D), jnp.float32, -1.0, 1.0), -1.0, 1.0),
        "w_query": scatter_about(splits[3], (D, D), D ** -0.5, 0.21875),
        "w_key": scatter_about(splits[4], (D, D), D ** -0.5, 0.21875),
        "w_value": scatter_about(splits[5], (D, D), D ** -0.5, 0.21875),
        "w_out": scatter_about(splits[6], (D, D), D ** -0.5, 0.21875),
        "live_counts": draw_live_counts(jax.random.fold_in(splits[8], 71), 0),
    }


def rounded(values_in):
    return lax.optimization_barrier(values_in.astype(jnp.bfloat16)).astype(jnp.float32)

def causal_conv(signal, kernel):
    length = signal.shape[1]
    padded = jnp.pad(signal, ((0, 0), (KW - 1, 0), (0, 0)))
    result = jnp.zeros_like(signal)
    for offset in range(KW):
        result = result + kernel[offset] * padded[:, KW - 1 - offset:KW - 1 - offset + length, :]
    return result

def conv_transpose(grads, kernel):
    length = grads.shape[1]
    padded = jnp.pad(grads, ((0, 0), (0, KW - 1), (0, 0)))
    result = jnp.zeros_like(grads)
    for offset in range(KW):
        result = result + kernel[offset] * padded[:, offset:offset + length, :]
    return result

def head_grads(operands):
    query_rows, key_rows, value_rows, grad_rows, key_mask = operands
    inv_root = 1.0 / math.sqrt(HD)
    logits = jnp.where(key_mask[None, :], jnp.dot(query_rows, key_rows.T) * inv_root, -1e+30)
    top_logit = lax.optimization_barrier(jnp.max(logits, axis=1, keepdims=True))
    log_total = top_logit + jnp.log(lax.optimization_barrier(jnp.sum(jnp.exp(logits - top_logit), axis=1, keepdims=True)))
    attention = jnp.exp(logits - log_total)
    weight_grad = jnp.dot(grad_rows, value_rows.T)
    row_delta = lax.optimization_barrier(jnp.sum(attention * weight_grad, axis=1, keepdims=True))
    score_grad = rounded(attention * (weight_grad - row_delta))
    query_grad = jnp.dot(score_grad, key_rows) * inv_root
    groups = N_REGION
    per_group = query_rows.shape[0] // groups
    key_count = key_rows.shape[0]
    key_part = jnp.einsum('gqk,gqd->gkd', score_grad.reshape(groups, per_group, key_count), query_rows.reshape(groups, per_group, HD)) * inv_root
    value_part = jnp.einsum('gqk,gqd->gkd', rounded(attention).reshape(groups, per_group, key_count), grad_rows.reshape(groups, per_group, HD))
    key_sum = rounded(lax.optimization_barrier(jnp.sum(rounded(key_part), axis=0)))
    value_sum = rounded(lax.optimization_barrier(jnp.sum(rounded(value_part), axis=0)))
    return (query_grad, key_sum, value_sum)

def make_span_grads(w_key, w_value):

    def span_grads(operands):
        query_rows, key_rows, value_rows, grad_rows, key_mask = operands

        def heads_first(array_in):
            return array_in.astype(jnp.float32).reshape(-1, H, HD).transpose(1, 0, 2)
        head_masks = jnp.broadcast_to(key_mask, (H, key_mask.shape[0]))
        query_part, key_sum, value_sum = lax.map(head_grads, (heads_first(query_rows), heads_first(key_rows), heads_first(value_rows), heads_first(grad_rows), head_masks))

        def flat_rows(array_in):
            return array_in.transpose(1, 0, 2).reshape(-1, H * HD).astype(jnp.bfloat16)
        side_grad = jnp.dot(flat_rows(key_sum), w_key.T, preferred_element_type=jnp.float32)
        side_grad = side_grad + jnp.dot(flat_rows(value_sum), w_value.T, preferred_element_type=jnp.float32)
        return (query_part.transpose(1, 0, 2).reshape(-1, H * HD), side_grad)
    return span_grads

def reference(latents, output_grad, conv_kernel, w_query, w_key, w_value, w_out, live_counts):
    regions, total_time, model_width = latents.shape
    hidden = causal_conv(latents.astype(jnp.float32), conv_kernel).astype(jnp.bfloat16)
    flattened = hidden.reshape(-1, model_width)
    queries = jnp.dot(flattened, w_query, preferred_element_type=jnp.float32).astype(jnp.bfloat16)
    key_proj = jnp.dot(flattened, w_key, preferred_element_type=jnp.float32).astype(jnp.bfloat16)
    value_proj = jnp.dot(flattened, w_value, preferred_element_type=jnp.float32).astype(jnp.bfloat16)
    position = lax.broadcasted_iota(jnp.int32, (regions, N_TM, TCH), 2)
    valid = position < live_counts[:, :, None]
    query_live = valid.reshape(regions * total_time, 1).astype(jnp.float32)
    grad_proj = (jnp.dot(output_grad.reshape(-1, model_width), w_out.T, preferred_element_type=jnp.float32) * query_live).astype(jnp.bfloat16)

    def by_span(array_in):
        return array_in.reshape(regions, N_TM, TCH, model_width).transpose(1, 0, 2, 3).reshape(N_TM, regions * TCH, model_width)
    key_mask = valid.transpose(1, 0, 2).reshape(N_TM, regions * TCH)
    query_part, side_part = lax.map(make_span_grads(w_key, w_value), (by_span(queries), by_span(key_proj), by_span(value_proj), by_span(grad_proj), key_mask))

    def by_region(array_in):
        return array_in.reshape(N_TM, regions, TCH, model_width).transpose(1, 0, 2, 3).reshape(-1, model_width)
    query_grad = by_region(query_part).astype(jnp.bfloat16)
    side_grad = by_region(side_part)
    hidden_grad = jnp.dot(query_grad, w_query.T, preferred_element_type=jnp.float32) + side_grad
    input_grad = conv_transpose(hidden_grad.reshape(regions, total_time, model_width), conv_kernel)
    return input_grad.astype(jnp.bfloat16)
```

```python
import functools
import math

import jax
import jax.numpy as jnp
from jax import lax
from jax.experimental import pallas as pl
from jax.experimental.pallas import tpu as pltpu
from jax.sharding import PartitionSpec as P

H = 12
HD = 64
KW = 4
WAYS = 2
BLOCK = 16
KEY_STEP = 256
QUERY_STEP = 256
MASKED = -1e30
VMEM_BYTES = 56 * 1024 * 1024
BF16 = jnp.bfloat16
F32 = jnp.float32


def passed_along(block, axis, distance):
    devices = range(lax.axis_size(axis))
    route = [(i - distance, i) for i in devices if i - distance in devices]
    return lax.ppermute(block, axis, route)


def times(left, right):
    return lax.dot_general(left, right, (((1,), (0,)), ((), ())), preferred_element_type=F32)


def times_back(left, right):
    return lax.dot_general(left, right, (((1,), (1,)), ((), ())), preferred_element_type=F32)


def vmem():
    return pl.BlockSpec(memory_space=pltpu.VMEM)


def smem():
    return pl.BlockSpec(memory_space=pltpu.SMEM)


def params():
    return pltpu.CompilerParams(vmem_limit_bytes=VMEM_BYTES)


def project_kernel(
    place_ref, latents_ref, edge_ref, grad_ref, taps_ref, wq_ref, wk_ref, wv_ref, wo_ref, send_ref, qg_ref
):
    span = latents_ref.shape[0]
    region, live = place_ref[0], place_ref[1]
    extended = jnp.concatenate([edge_ref[...].astype(F32), latents_ref[...].astype(F32)], axis=0)
    convolved = jnp.zeros(latents_ref.shape, F32)
    for offset in range(KW):
        start = KW - 1 - offset
        convolved = convolved + taps_ref[offset : offset + 1, :] * extended[start : start + span, :]
    hidden = convolved.astype(BF16)
    rows = lax.broadcasted_iota(jnp.int32, (span, 1), 0)
    alive = (rows < live).astype(F32)
    grads = (times_back(grad_ref[...], wo_ref[...]) * alive).astype(BF16)
    queries = (times(hidden, wq_ref[...]).astype(BF16).astype(F32) * (1.0 / math.sqrt(HD))).astype(BF16)
    keys = times(hidden, wk_ref[...]).astype(BF16)
    values = times(hidden, wv_ref[...]).astype(BF16)
    count = jnp.zeros((BLOCK, 2 * HD), F32) + live.astype(F32)
    count = count.astype(BF16)
    for head in range(H):
        cut = slice(head * HD, (head + 1) * HD)
        pair = jnp.concatenate([keys[:, cut], values[:, cut]], axis=1)
        qg_ref[...] = jnp.concatenate([queries[:, cut], grads[:, cut]], axis=1)
        for half in range(WAYS):
            send_ref[head * WAYS + half, :span, :] = pair
            send_ref[head * WAYS + half, span + span // WAYS :, :] = count
        for block in range(span // BLOCK):
            half = lax.rem(block + region, WAYS)
            to = span + (block // WAYS) * BLOCK
            send_ref[head * WAYS + half, to : to + BLOCK, :] = qg_ref[block * BLOCK : (block + 1) * BLOCK, :]


def attend_kernel(
    place_ref,
    recv_ref,
    send_ref,
    kaug_ref,
    kv_ref,
    kt_ref,
    qg_ref,
    qa_ref,
    gm_ref,
    p_ref,
    wg_ref,
    top_ref,
    dkv_ref,
    dq_ref,
    koff_ref,
    qoff_ref,
):
    regions = recv_ref.shape[0]
    span = kv_ref.shape[0] // regions
    share = span // WAYS
    me = place_ref[0]
    half = lax.rem(me, WAYS)
    busy = me < H * WAYS
    lane_k = lax.broadcasted_iota(jnp.int32, (span, 2 * HD), 1)
    row_k = lax.broadcasted_iota(jnp.int32, (span, 2 * HD), 0)
    lane_q = lax.broadcasted_iota(jnp.int32, (share, 2 * HD), 1)

    @pl.when(busy)
    def _():
        lane = lax.broadcasted_iota(jnp.int32, (KEY_STEP, 2 * HD), 1)
        blank = jnp.where(lane == HD, MASKED, 0.0).astype(BF16)
        none = jnp.zeros((KEY_STEP, 2 * HD), BF16)
        for step in range(kaug_ref.shape[0] // KEY_STEP):
            kaug_ref[step * KEY_STEP : (step + 1) * KEY_STEP, :] = blank
            kv_ref[step * KEY_STEP : (step + 1) * KEY_STEP, :] = none
            dkv_ref[step * KEY_STEP : (step + 1) * KEY_STEP, :] = jnp.zeros((KEY_STEP, 2 * HD), F32)
        for step in range(qg_ref.shape[0] // QUERY_STEP):
            qg_ref[step * QUERY_STEP : (step + 1) * QUERY_STEP, :] = none
            qa_ref[step * QUERY_STEP : (step + 1) * QUERY_STEP, :] = none
            gm_ref[step * QUERY_STEP : (step + 1) * QUERY_STEP, :] = none

    def compact(region, totals):
        key_at, query_at = totals
        koff_ref[region] = key_at
        qoff_ref[region] = query_at
        live = jnp.max(recv_ref[region, span + share :, :].astype(F32)).astype(jnp.int32)
        live = jnp.where(busy, jnp.clip(live, 0, span), 0)
        blocks = lax.div(live + BLOCK - 1, BLOCK)
        pair = recv_ref[region, :span, :].astype(F32)
        kv_ref[pl.ds(pl.multiple_of(key_at, BLOCK), span), :] = pair.astype(BF16)
        bias = jnp.where(row_k < live, 0.0, MASKED)
        kaug = jnp.where(lane_k < HD, pair, jnp.where(lane_k == HD, bias, 0.0))
        kaug_ref[pl.ds(pl.multiple_of(key_at, BLOCK), span), :] = kaug.astype(BF16)
        both = recv_ref[region, span : span + share, :].astype(F32)
        to = pl.ds(pl.multiple_of(query_at, BLOCK), share)
        qg_ref[to, :] = both.astype(BF16)
        qa_ref[to, :] = jnp.where(lane_q < HD, both, jnp.where(lane_q == HD, 1.0, 0.0)).astype(BF16)
        gm_ref[to, :] = jnp.where(lane_q >= HD, both, 0.0).astype(BF16)
        mine = lax.div(blocks + 1 - lax.rem(half + region, WAYS), WAYS)
        return (key_at + blocks * BLOCK, query_at + mine * BLOCK)

    zero = jnp.int32(0)
    key_total, query_total = lax.fori_loop(0, regions, compact, (zero, zero))
    key_steps = lax.div(key_total + KEY_STEP - 1, KEY_STEP)
    query_steps = lax.div(query_total + QUERY_STEP - 1, QUERY_STEP)

    def turn(step, carry):
        keys = kaug_ref[pl.ds(pl.multiple_of(step * KEY_STEP, KEY_STEP), KEY_STEP), :]
        kt_ref[step] = keys.astype(F32).T[:HD, :].astype(BF16)
        return carry

    lax.fori_loop(0, key_steps, turn, 0)

    def query_block(block, carry):
        at = pl.ds(pl.multiple_of(block * QUERY_STEP, QUERY_STEP), QUERY_STEP)

        def gather(step, state):
            top, total, dot = state
            here = pl.ds(pl.multiple_of(step * KEY_STEP, KEY_STEP), KEY_STEP)
            logits = times_back(kaug_ref[here, :], qa_ref[at, :]).reshape(KEY_STEP // 8, 8, QUERY_STEP)
            weight_grad = times_back(kv_ref[here, :], gm_ref[at, :]).reshape(KEY_STEP // 8, 8, QUERY_STEP)
            new_top = jnp.maximum(top, jnp.max(logits, axis=0))
            shrink = jnp.exp(top - new_top)
            raised = jnp.exp(logits - new_top[None])
            p_ref[step] = raised
            wg_ref[step] = weight_grad
            top_ref[step] = new_top
            total = total * shrink + jnp.sum(raised, axis=0)
            dot = dot * shrink + jnp.sum(raised * weight_grad, axis=0)
            return (new_top, total, dot)

        none = jnp.zeros((8, QUERY_STEP), F32)
        top, total, dot = lax.fori_loop(0, key_steps, gather, (none + MASKED, none, none))
        best = jnp.max(top, axis=0, keepdims=True)
        shrink = jnp.exp(top - best)
        whole = jnp.sum(total * shrink, axis=0, keepdims=True)
        inverse = 1.0 / whole
        delta = jnp.sum(dot * shrink, axis=0, keepdims=True) * inverse

        def spread(step, query_grad):
            here = pl.ds(pl.multiple_of(step * KEY_STEP, KEY_STEP), KEY_STEP)
            factor = jnp.exp(top_ref[step] - best) * inverse
            attention = p_ref[step] * factor[None]
            score_grad = attention * (wg_ref[step] - delta[None])
            attention = attention.reshape(KEY_STEP, QUERY_STEP).astype(BF16)
            score_grad = score_grad.reshape(KEY_STEP, QUERY_STEP).astype(BF16)
            both = qg_ref[at, :]
            lane = lax.broadcasted_iota(jnp.int32, (KEY_STEP, 2 * HD), 1)
            dkv_ref[here, :] += jnp.where(lane < HD, times(score_grad, both), times(attention, both))
            return query_grad + times(kt_ref[step], score_grad)

        query_grad = lax.fori_loop(0, key_steps, spread, jnp.zeros((HD, QUERY_STEP), F32))
        query_grad = query_grad * (1.0 / math.sqrt(HD))
        dq_ref[at, :] = jnp.concatenate([query_grad, query_grad], axis=0).T
        return carry

    lax.fori_loop(0, query_steps, query_block, 0)

    def give_back(region, carry):
        here = pl.ds(pl.multiple_of(koff_ref[region], BLOCK), span)
        send_ref[region, :span, :] = dkv_ref[here, :].astype(BF16)
        first = dq_ref[pl.ds(pl.multiple_of(qoff_ref[region], BLOCK), share // 2), :]
        second = dq_ref[pl.ds(pl.multiple_of(qoff_ref[region] + share // 2, BLOCK), share // 2), :]
        lane = lax.broadcasted_iota(jnp.int32, (share // 2, 2 * HD), 1)
        send_ref[region, span:, :] = jnp.where(lane < HD, first, second).astype(BF16)
        return carry

    lax.fori_loop(0, regions, give_back, 0)


def return_kernel(place_ref, recv_ref, wq_ref, wk_ref, wv_ref, hidden_grad_ref, dk_ref, dv_ref, dq_ref):
    span = hidden_grad_ref.shape[0]
    quarter = span // WAYS // 2
    region, live = place_ref[0], place_ref[1]
    alive = lax.broadcasted_iota(jnp.int32, (span, 1), 0) < live
    for duo in range(H // 2):
        cut = slice(duo * 2 * HD, (duo + 1) * 2 * HD)
        left, right = 2 * duo * WAYS, (2 * duo + 1) * WAYS
        first = recv_ref[left, :span, :].astype(F32) + recv_ref[left + 1, :span, :].astype(F32)
        second = recv_ref[right, :span, :].astype(F32) + recv_ref[right + 1, :span, :].astype(F32)
        key_grad = jnp.concatenate([first[:, :HD], second[:, :HD]], axis=1)
        value_grad = jnp.concatenate([first[:, HD:], second[:, HD:]], axis=1)
        dk_ref[:, cut] = jnp.where(alive, key_grad, 0.0).astype(BF16)
        dv_ref[:, cut] = jnp.where(alive, value_grad, 0.0).astype(BF16)
        for half in range(WAYS):
            shift = lax.rem(half + region, WAYS)
            one = recv_ref[left + half, span:, :].astype(F32)
            two = recv_ref[right + half, span:, :].astype(F32)
            low = jnp.concatenate([one[:, :HD], two[:, :HD]], axis=1)
            high = jnp.concatenate([one[:, HD:], two[:, HD:]], axis=1)
            for number, part in enumerate((low, high)):
                for piece in range(quarter // BLOCK):
                    index = number * (quarter // BLOCK) + piece
                    to = pl.multiple_of((WAYS * index + shift) * BLOCK, BLOCK)
                    dq_ref[pl.ds(to, BLOCK), cut] = part[piece * BLOCK : (piece + 1) * BLOCK, :]
    query_grad = jnp.where(alive, dq_ref[...], 0.0).astype(BF16)
    hidden_grad_ref[...] = times_back(query_grad, wq_ref[...]) + (
        times_back(dk_ref[...], wk_ref[...]) + times_back(dv_ref[...], wv_ref[...])
    )


def shards(latents, output_grad, conv_kernel, w_query, w_key, w_value, w_out, live_counts):
    _, span, width = latents.shape
    regions = lax.axis_size("region")
    share = span // WAYS
    region = lax.axis_index("region").astype(jnp.int32)
    place = jnp.stack([region, live_counts[0, 0]])
    edge = passed_along(latents[:, span - (KW - 1) :, :], "tm", 1)
    sent = pl.pallas_call(
        project_kernel,
        name="project",
        out_shape=jax.ShapeDtypeStruct((regions, span + share + BLOCK, 2 * HD), BF16),
        in_specs=[smem()] + [vmem()] * 8,
        out_specs=vmem(),
        scratch_shapes=[pltpu.VMEM((span, 2 * HD), BF16)],
        compiler_params=params(),
    )(place, latents[0], edge[0], output_grad[0], conv_kernel, w_query, w_key, w_value, w_out)
    gathered = lax.all_to_all(sent, "region", 0, 0, tiled=True)
    keys, queries = regions * span, regions * share
    key_steps = keys // KEY_STEP
    grads = pl.pallas_call(
        attend_kernel,
        name="attend",
        out_shape=jax.ShapeDtypeStruct((regions, span + share // 2, 2 * HD), BF16),
        in_specs=[smem(), vmem()],
        out_specs=vmem(),
        scratch_shapes=[
            pltpu.VMEM((keys, 2 * HD), BF16),
            pltpu.VMEM((keys, 2 * HD), BF16),
            pltpu.VMEM((key_steps, HD, KEY_STEP), BF16),
            pltpu.VMEM((queries, 2 * HD), BF16),
            pltpu.VMEM((queries, 2 * HD), BF16),
            pltpu.VMEM((queries, 2 * HD), BF16),
            pltpu.VMEM((key_steps, KEY_STEP // 8, 8, QUERY_STEP), F32),
            pltpu.VMEM((key_steps, KEY_STEP // 8, 8, QUERY_STEP), F32),
            pltpu.VMEM((key_steps, 8, QUERY_STEP), F32),
            pltpu.VMEM((keys, 2 * HD), F32),
            pltpu.VMEM((queries, 2 * HD), F32),
            pltpu.SMEM((regions,), jnp.int32),
            pltpu.SMEM((regions,), jnp.int32),
        ],
        compiler_params=params(),
    )(place, gathered)
    returned = lax.all_to_all(grads, "region", 0, 0, tiled=True)
    hidden_grad = pl.pallas_call(
        return_kernel,
        name="project_back",
        out_shape=jax.ShapeDtypeStruct((span, width), F32),
        in_specs=[smem()] + [vmem()] * 4,
        out_specs=vmem(),
        scratch_shapes=[
            pltpu.VMEM((span, width), BF16),
            pltpu.VMEM((span, width), BF16),
            pltpu.VMEM((span, width), F32),
        ],
        compiler_params=params(),
    )(place, returned, w_query, w_key, w_value)
    grad_cube = hidden_grad[None]
    later_rows = passed_along(grad_cube[:, : KW - 1, :], "tm", -1)
    grad_extended = jnp.concatenate([grad_cube, later_rows], axis=1)
    input_grad = jnp.zeros((1, span, width), F32)
    for offset in range(KW):
        input_grad = input_grad + conv_kernel[offset] * grad_extended[:, offset : offset + span, :]
    return input_grad.astype(BF16)


def solution(mesh):
    in_specs = (
        P("region", "tm", None),
        P("region", "tm", None),
        P(),
        P(),
        P(),
        P(),
        P(),
        P("region", "tm"),
    )
    out_specs = P("region", "tm", None)
    return jax.shard_map(shards, mesh=mesh, in_specs=in_specs, out_specs=out_specs, check_vma=False)
```

```python
import math

import jax
import jax.numpy as jnp
from jax import lax
from jax.experimental import pallas as pl
from jax.experimental.pallas import tpu as pltpu
from jax.sharding import PartitionSpec as P

H = 12
HD = 64
KW = 4
WAYS = 2
BLOCK = 16
KEY_STEP = 512
QUERY_STEP = 1024
QUERY_WIDTHS = (512, 768, 1024)
MASKED = -1e30
HEADS_STEP = 4
BF16 = jnp.bfloat16
F32 = jnp.float32


def passed_along(block, axis, distance):
    devices = range(lax.axis_size(axis))
    route = [(i - distance, i) for i in devices if i - distance in devices]
    return lax.ppermute(block, axis, route)


def times(left, right):
    return lax.dot_general(left, right, (((1,), (0,)), ((), ())), preferred_element_type=F32)


def times_back(left, right):
    return lax.dot_general(left, right, (((1,), (1,)), ((), ())), preferred_element_type=F32)


def vmem():
    return pl.BlockSpec(memory_space=pltpu.VMEM)


def smem():
    return pl.BlockSpec(memory_space=pltpu.SMEM)


def fixed(*shape):
    return pl.BlockSpec(shape, lambda i: (0,) * len(shape))


def params(mebibytes):
    return pltpu.CompilerParams(vmem_limit_bytes=mebibytes * 1024 * 1024)


def project_kernel(
    region_ref, live_ref, latents_ref, edge_ref, grad_ref, taps_ref, wq_ref, wk_ref, wv_ref, wo_ref, send_ref,
    hidden_ref, qg_ref
):
    span = latents_ref.shape[0]
    region, live = region_ref[0], live_ref[0, 0]

    @pl.when(pl.program_id(0) == 0)
    def _():
        extended = jnp.concatenate([edge_ref[...].astype(F32), latents_ref[...].astype(F32)], axis=0)
        convolved = jnp.zeros(latents_ref.shape, F32)
        for offset in range(KW):
            start = KW - 1 - offset
            convolved = convolved + taps_ref[offset : offset + 1, :] * extended[start : start + span, :]
        hidden_ref[...] = convolved.astype(BF16)

    hidden = hidden_ref[...]
    rows = lax.broadcasted_iota(jnp.int32, (span, 1), 0)
    alive = (rows < live).astype(F32)
    grads = (times_back(grad_ref[...], wo_ref[...]) * alive).astype(BF16)
    queries = (times(hidden, wq_ref[...]).astype(BF16).astype(F32) * (1.0 / math.sqrt(HD))).astype(BF16)
    keys = times(hidden, wk_ref[...]).astype(BF16)
    values = times(hidden, wv_ref[...]).astype(BF16)
    count = (jnp.zeros((BLOCK, 2 * HD), F32) + live.astype(F32)).astype(BF16)
    for head in range(HEADS_STEP):
        cut = slice(head * HD, (head + 1) * HD)
        pair = jnp.concatenate([keys[:, cut], values[:, cut]], axis=1)
        qg_ref[head] = jnp.concatenate([queries[:, cut], grads[:, cut]], axis=1)
        for half in range(WAYS):
            send_ref[head * WAYS + half, :span, :] = pair
            send_ref[head * WAYS + half, span + span // WAYS :, :] = count
        for block in range(span // BLOCK):
            half = lax.rem(block + region, WAYS)
            to = span + (block // WAYS) * BLOCK
            send_ref[head * WAYS + half, to : to + BLOCK, :] = qg_ref[head, block * BLOCK : (block + 1) * BLOCK, :]


def attend_kernel(
    region_ref,
    recv_ref,
    send_ref,
    kaug_ref,
    kv_ref,
    kt_ref,
    qg_ref,
    qa_ref,
    gm_ref,
    p_ref,
    wg_ref,
    top_ref,
    dkv_ref,
    dq_ref,
    koff_ref,
    qoff_ref,
):
    regions = recv_ref.shape[0]
    share = (recv_ref.shape[1] - BLOCK) // (WAYS + 1)
    span = share * WAYS
    me = region_ref[0]
    half = lax.rem(me, WAYS)
    busy = me < H * WAYS
    lane = lax.broadcasted_iota(jnp.int32, (BLOCK, 2 * HD), 1)
    row = lax.broadcasted_iota(jnp.int32, (BLOCK, 2 * HD), 0)
    low = (lax.broadcasted_iota(jnp.int32, (1, 2 * HD), 1) < HD).astype(BF16)
    high = (lax.broadcasted_iota(jnp.int32, (1, 2 * HD), 1) >= HD).astype(BF16)
    mark = (lax.broadcasted_iota(jnp.int32, (1, 2 * HD), 1) == HD).astype(BF16)
    lives = []
    for region in range(regions):
        live = jnp.max(recv_ref[region, span + share :, :].astype(F32)).astype(jnp.int32)
        lives.append(jnp.where(busy, jnp.clip(live, 0, span), 0))
    key_total = query_total = jnp.int32(0)
    for region in range(regions):
        live = lives[region]
        koff_ref[region] = key_total
        qoff_ref[region] = query_total
        pair = recv_ref[region, :span, :]
        here = pl.ds(pl.multiple_of(key_total, BLOCK), span)
        kv_ref[here, :] = pair
        kaug_ref[here, :] = pair * low
        whole = lax.div(live, BLOCK)
        edge = pl.ds(pl.multiple_of(key_total + whole * BLOCK, BLOCK), BLOCK)
        bias = jnp.where((lane == HD) & (row >= live - whole * BLOCK), MASKED, 0.0).astype(BF16)
        kaug_ref[edge, :] += bias
        both = recv_ref[region, span : span + share, :]
        to = pl.ds(pl.multiple_of(query_total, BLOCK), share)
        qg_ref[to, :] = both
        qa_ref[to, :] = both * low + mark
        gm_ref[to, :] = both * high
        blocks = lax.div(live + BLOCK - 1, BLOCK)
        mine = lax.div(blocks + 1 - lax.rem(half + region, WAYS), WAYS)
        key_total += blocks * BLOCK
        query_total += mine * BLOCK
    rest = pl.ds(pl.multiple_of(key_total, BLOCK), KEY_STEP)
    none = jnp.zeros((KEY_STEP, 2 * HD), BF16)
    kv_ref[rest, :] = none
    kaug_ref[rest, :] = none + mark * MASKED
    rest = pl.ds(pl.multiple_of(query_total, BLOCK), QUERY_STEP)
    none = jnp.zeros((QUERY_STEP, 2 * HD), BF16)
    qg_ref[rest, :] = none
    qa_ref[rest, :] = none
    gm_ref[rest, :] = none
    key_steps = lax.div(key_total + KEY_STEP - 1, KEY_STEP)

    def turn(step, carry):
        keys = kaug_ref[pl.ds(pl.multiple_of(step * KEY_STEP, KEY_STEP), KEY_STEP), :]
        dkv_ref[pl.ds(pl.multiple_of(step * KEY_STEP, KEY_STEP), KEY_STEP), :] = jnp.zeros((KEY_STEP, 2 * HD), F32)
        kt_ref[step] = keys.astype(F32).T[:HD, :].astype(BF16)
        return carry

    lax.fori_loop(0, key_steps, turn, 0)

    def query_block(start, wide):
        at = pl.ds(pl.multiple_of(start, BLOCK), wide)

        def gather(step, state):
            top, total, dot = state
            here = pl.ds(pl.multiple_of(step * KEY_STEP, KEY_STEP), KEY_STEP)
            logits = times_back(kaug_ref[here, :], qa_ref[at, :]).reshape(KEY_STEP // 8, 8, wide)
            weight_grad = times_back(kv_ref[here, :], gm_ref[at, :]).reshape(KEY_STEP // 8, 8, wide)
            new_top = jnp.maximum(top, jnp.max(logits, axis=0))
            shrink = jnp.exp(top - new_top)
            raised = jnp.exp(logits - new_top[None])
            p_ref[step, :, :, :wide] = raised
            wg_ref[step, :, :, :wide] = weight_grad
            top_ref[step, :, :wide] = new_top
            total = total * shrink + jnp.sum(raised, axis=0)
            dot = dot * shrink + jnp.sum(raised * weight_grad, axis=0)
            return (new_top, total, dot)

        none = jnp.zeros((8, wide), F32)
        top, total, dot = lax.fori_loop(0, key_steps, gather, (none + MASKED, none, none))
        best = jnp.max(top, axis=0, keepdims=True)
        shrink = jnp.exp(top - best)
        whole = jnp.sum(total * shrink, axis=0, keepdims=True)
        inverse = 1.0 / whole
        delta = jnp.sum(dot * shrink, axis=0, keepdims=True) * inverse

        def spread(step, query_grad):
            here = pl.ds(pl.multiple_of(step * KEY_STEP, KEY_STEP), KEY_STEP)
            factor = jnp.exp(top_ref[step, :, :wide] - best) * inverse
            attention = p_ref[step, :, :, :wide] * factor[None]
            score_grad = attention * (wg_ref[step, :, :, :wide] - delta[None])
            attention = attention.reshape(KEY_STEP, wide).astype(BF16)
            score_grad = score_grad.reshape(KEY_STEP, wide).astype(BF16)
            both = qg_ref[at, :]
            lane = lax.broadcasted_iota(jnp.int32, (KEY_STEP, 2 * HD), 1)
            dkv_ref[here, :] += jnp.where(lane < HD, times(score_grad, both), times(attention, both))
            return query_grad + times(kt_ref[step], score_grad)

        query_grad = lax.fori_loop(0, key_steps, spread, jnp.zeros((HD, wide), F32))
        query_grad = query_grad * (1.0 / math.sqrt(HD))
        dq_ref[at, :] = jnp.concatenate([query_grad, query_grad], axis=0).T

    full = lax.div(query_total, QUERY_STEP)
    left = query_total - full * QUERY_STEP
    for index, wide in enumerate(QUERY_WIDTHS):
        above = QUERY_WIDTHS[index - 1] if index else 0

        @pl.when((left > above) & (left <= wide))
        def _(wide=wide):
            query_block(full * QUERY_STEP, wide)

    def whole_block(block, carry):
        query_block(block * QUERY_STEP, QUERY_STEP)
        return carry

    lax.fori_loop(0, full, whole_block, 0)

    lane = lax.broadcasted_iota(jnp.int32, (share // 2, 2 * HD), 1)
    for region in range(regions):
        here = pl.ds(pl.multiple_of(koff_ref[region], BLOCK), span)
        send_ref[region, :span, :] = dkv_ref[here, :].astype(BF16)
        first = dq_ref[pl.ds(pl.multiple_of(qoff_ref[region], BLOCK), share // 2), :]
        second = dq_ref[pl.ds(pl.multiple_of(qoff_ref[region] + share // 2, BLOCK), share // 2), :]
        send_ref[region, span:, :] = jnp.where(lane < HD, first, second).astype(BF16)


def return_kernel(
    region_ref, live_ref, recv_ref, taps_ref, wq_ref, wk_ref, wv_ref, out_ref, first_ref, last_ref,
    dk_ref, dv_ref, dq_ref, total_ref
):
    span, width = total_ref.shape[0] - 8, total_ref.shape[1]
    quarter = span // WAYS // 2
    region, live = region_ref[0], live_ref[0, 0]
    alive = lax.broadcasted_iota(jnp.int32, (span, 1), 0) < live
    for duo in range(HEADS_STEP // 2):
        cut = slice(duo * 2 * HD, (duo + 1) * 2 * HD)
        left, right = 2 * duo * WAYS, (2 * duo + 1) * WAYS
        first = recv_ref[left, :span, :].astype(F32) + recv_ref[left + 1, :span, :].astype(F32)
        second = recv_ref[right, :span, :].astype(F32) + recv_ref[right + 1, :span, :].astype(F32)
        key_grad = jnp.concatenate([first[:, :HD], second[:, :HD]], axis=1)
        value_grad = jnp.concatenate([first[:, HD:], second[:, HD:]], axis=1)
        dk_ref[:, cut] = jnp.where(alive, key_grad, 0.0).astype(BF16)
        dv_ref[:, cut] = jnp.where(alive, value_grad, 0.0).astype(BF16)
        for half in range(WAYS):
            shift = lax.rem(half + region, WAYS)
            one = recv_ref[left + half, span:, :].astype(F32)
            two = recv_ref[right + half, span:, :].astype(F32)
            low = jnp.concatenate([one[:, :HD], two[:, :HD]], axis=1)
            high = jnp.concatenate([one[:, HD:], two[:, HD:]], axis=1)
            for number, part in enumerate((low, high)):
                for piece in range(quarter // BLOCK):
                    index = number * (quarter // BLOCK) + piece
                    to = pl.multiple_of((WAYS * index + shift) * BLOCK, BLOCK)
                    dq_ref[pl.ds(to, BLOCK), cut] = part[piece * BLOCK : (piece + 1) * BLOCK, :]
    query_grad = jnp.where(alive, dq_ref[...], 0.0).astype(BF16)
    term = times_back(query_grad, wq_ref[...]) + (
        times_back(dk_ref[...], wk_ref[...]) + times_back(dv_ref[...], wv_ref[...])
    )
    step = pl.program_id(0)

    @pl.when(step == 0)
    def _():
        total_ref[:span, :] = term

    @pl.when(step > 0)
    def _():
        total_ref[:span, :] += term

    @pl.when(step == pl.num_programs(0) - 1)
    def _():
        total_ref[span:, :] = jnp.zeros((8, width), F32)
        input_grad = jnp.zeros((span, width), F32)
        for offset in range(KW):
            input_grad = input_grad + taps_ref[offset : offset + 1, :] * total_ref[offset : offset + span, :]
        out_ref[...] = input_grad.astype(BF16)
        last_ref[...] = input_grad[span - BLOCK :, :]
        first_ref[...] = total_ref[:8, :]


def finish_kernel(last_ref, later_ref, taps_ref, whole_ref, out_ref):
    del whole_ref
    rows, width = last_ref.shape
    total = last_ref[...]
    for offset in range(1, KW):
        reach = jnp.concatenate([jnp.zeros((rows - offset, width), F32), later_ref[:offset, :]], axis=0)
        total = total + taps_ref[offset : offset + 1, :] * reach
    out_ref[...] = total.astype(BF16)


def attend_call(region, gathered):
    regions, rows, _ = gathered.shape
    share = (rows - BLOCK) // (WAYS + 1)
    span = share * WAYS
    keys, queries = regions * span, regions * share
    key_steps = -(-keys // KEY_STEP)
    return pl.pallas_call(
        attend_kernel,
        name="attend",
        out_shape=jax.ShapeDtypeStruct((regions, span + share // 2, 2 * HD), BF16),
        in_specs=[smem(), vmem()],
        out_specs=vmem(),
        scratch_shapes=[
            pltpu.VMEM((keys + KEY_STEP, 2 * HD), BF16),
            pltpu.VMEM((keys + KEY_STEP, 2 * HD), BF16),
            pltpu.VMEM((key_steps, HD, KEY_STEP), BF16),
            pltpu.VMEM((queries + QUERY_STEP, 2 * HD), BF16),
            pltpu.VMEM((queries + QUERY_STEP, 2 * HD), BF16),
            pltpu.VMEM((queries + QUERY_STEP, 2 * HD), BF16),
            pltpu.VMEM((key_steps, KEY_STEP // 8, 8, QUERY_STEP), F32),
            pltpu.VMEM((key_steps, KEY_STEP // 8, 8, QUERY_STEP), F32),
            pltpu.VMEM((key_steps, 8, QUERY_STEP), F32),
            pltpu.VMEM((keys + KEY_STEP, 2 * HD), F32),
            pltpu.VMEM((queries + QUERY_STEP, 2 * HD), F32),
            pltpu.SMEM((regions,), jnp.int32),
            pltpu.SMEM((regions,), jnp.int32),
        ],
        compiler_params=params(50),
    )(region, gathered)


def shards(latents, output_grad, conv_kernel, w_query, w_key, w_value, w_out, live_counts):
    _, span, width = latents.shape
    regions = lax.axis_size("region")
    share = span // WAYS
    region = lax.axis_index("region").astype(jnp.int32).reshape(1)
    edge = passed_along(latents[:, span - (KW - 1) :, :], "tm", 1)
    steps = H // HEADS_STEP
    columns = HEADS_STEP * HD
    by_columns = pl.BlockSpec((width, columns), lambda i: (0, i))
    sent = pl.pallas_call(
        project_kernel,
        name="project",
        grid=(steps,),
        out_shape=jax.ShapeDtypeStruct((regions, span + share + BLOCK, 2 * HD), BF16),
        in_specs=[
            smem(),
            smem(),
            fixed(span, width),
            fixed(KW - 1, width),
            fixed(span, width),
            fixed(KW, width),
            by_columns,
            by_columns,
            by_columns,
            pl.BlockSpec((columns, width), lambda i: (i, 0)),
        ],
        out_specs=pl.BlockSpec((HEADS_STEP * WAYS, span + share + BLOCK, 2 * HD), lambda i: (i, 0, 0)),
        scratch_shapes=[pltpu.VMEM((span, width), BF16), pltpu.VMEM((HEADS_STEP, span, 2 * HD), BF16)],
        compiler_params=params(60),
    )(region, live_counts, latents[0], edge[0], output_grad[0], conv_kernel, w_query, w_key, w_value, w_out)
    gathered = lax.all_to_all(sent, "region", 0, 0, tiled=True)
    grads = attend_call(region, gathered)
    returned = lax.all_to_all(grads, "region", 0, 0, tiled=True)
    partial, first, last = pl.pallas_call(
        return_kernel,
        name="project_back",
        grid=(steps,),
        out_shape=(
            jax.ShapeDtypeStruct((span, width), BF16),
            jax.ShapeDtypeStruct((8, width), F32),
            jax.ShapeDtypeStruct((BLOCK, width), F32),
        ),
        in_specs=[
            smem(),
            smem(),
            pl.BlockSpec((HEADS_STEP * WAYS, span + share // 2, 2 * HD), lambda i: (i, 0, 0)),
            fixed(KW, width),
            by_columns,
            by_columns,
            by_columns,
        ],
        out_specs=(fixed(span, width), fixed(8, width), fixed(BLOCK, width)),
        scratch_shapes=[
            pltpu.VMEM((span, columns), BF16),
            pltpu.VMEM((span, columns), BF16),
            pltpu.VMEM((span, columns), F32),
            pltpu.VMEM((span + 8, width), F32),
        ],
        compiler_params=params(16),
    )(region, live_counts, returned, conv_kernel, w_query, w_key, w_value)
    later = passed_along(first, "tm", -1)
    input_grad = pl.pallas_call(
        finish_kernel,
        name="finish",
        grid=(1,),
        out_shape=jax.ShapeDtypeStruct((span, width), BF16),
        in_specs=[
            fixed(BLOCK, width),
            fixed(8, width),
            fixed(KW, width),
            pl.BlockSpec(memory_space=pl.ANY),
        ],
        out_specs=pl.BlockSpec((BLOCK, width), lambda i: (span // BLOCK - 1, 0)),
        input_output_aliases={3: 0},
        compiler_params=params(4),
    )(last, later, conv_kernel, partial)
    return input_grad[None]


def solution(mesh):
    in_specs = (
        P("region", "tm", None),
        P("region", "tm", None),
        P(),
        P(),
        P(),
        P(),
        P(),
        P("region", "tm"),
    )
    out_specs = P("region", "tm", None)
    return jax.shard_map(shards, mesh=mesh, in_specs=in_specs, out_specs=out_specs, check_vma=False)
```

```python
import math

import jax
import jax.numpy as jnp
from jax import lax
from jax.experimental import pallas as pl
from jax.experimental.pallas import tpu as pltpu
from jax.sharding import PartitionSpec as P

H = 12
HD = 64
KW = 4
WAYS = 2
BLOCK = 16
KEY_STEP = 512
QUERY_STEP = 1024
QUERY_WIDTHS = (512, 768, 1024)
MASKED = -1e30
HEADS_STEP = 4
BF16 = jnp.bfloat16
F32 = jnp.float32


def passed_along(block, axis, distance):
    devices = range(lax.axis_size(axis))
    route = [(i - distance, i) for i in devices if i - distance in devices]
    return lax.ppermute(block, axis, route)


def times(left, right):
    return lax.dot_general(left, right, (((1,), (0,)), ((), ())), preferred_element_type=F32)


def times_back(left, right):
    return lax.dot_general(left, right, (((1,), (1,)), ((), ())), preferred_element_type=F32)


def vmem():
    return pl.BlockSpec(memory_space=pltpu.VMEM)


def smem():
    return pl.BlockSpec(memory_space=pltpu.SMEM)


def fixed(*shape):
    return pl.BlockSpec(shape, lambda i: (0,) * len(shape))


def params(mebibytes):
    return pltpu.CompilerParams(vmem_limit_bytes=mebibytes * 1024 * 1024)


def project_kernel(
    region_ref, live_ref, latents_hbm, edge_hbm, grad_hbm, taps_hbm, wq_hbm, wk_hbm, wv_hbm, wo_hbm, send_hbm,
    latents_ref, edge_ref, grad_ref, taps_ref, wq_ref, wk_ref, wv_ref, wo_ref, send_ref, qg_ref, in_sems, out_sems
):
    span = latents_ref.shape[0]
    columns = HEADS_STEP * HD
    dests = HEADS_STEP * WAYS
    steps = H // HEADS_STEP
    region, live = region_ref[0], live_ref[0, 0]
    small = [
        pltpu.make_async_copy(source, target, in_sems.at[index])
        for index, (source, target) in enumerate(
            ((latents_hbm, latents_ref), (edge_hbm, edge_ref), (taps_hbm, taps_ref), (grad_hbm, grad_ref))
        )
    ]
    weights = []
    for step in range(steps):
        cut = slice(step * columns, (step + 1) * columns)
        parts = [(source.at[:, cut], target.at[step]) for source, target in ((wq_hbm, wq_ref), (wk_hbm, wk_ref), (wv_hbm, wv_ref))]
        parts.append((wo_hbm.at[cut, :], wo_ref.at[step]))
        weights.append(
            [pltpu.make_async_copy(*part, in_sems.at[4 + 4 * step + index]) for index, part in enumerate(parts)]
        )
    for move in small:
        move.start()
    for group in weights:
        for move in group:
            move.start()
    for move in small[:3]:
        move.wait()
    extended = jnp.concatenate([edge_ref[...].astype(F32), latents_ref[...].astype(F32)], axis=0)
    convolved = jnp.zeros(latents_ref.shape, F32)
    for offset in range(KW):
        start = KW - 1 - offset
        convolved = convolved + taps_ref[offset : offset + 1, :] * extended[start : start + span, :]
    hidden = convolved.astype(BF16)
    alive = lax.broadcasted_iota(jnp.int32, (span, 1), 0) < live
    small[3].wait()
    given = grad_ref[...]
    leaving = []
    for step in range(steps):
        for move in weights[step]:
            move.wait()
        queries = (times(hidden, wq_ref[step]).astype(BF16).astype(F32) * (1.0 / math.sqrt(HD))).astype(BF16)
        keys = jnp.where(alive, times(hidden, wk_ref[step]), jnp.nan).astype(BF16)
        values = jnp.where(alive, times(hidden, wv_ref[step]), jnp.nan).astype(BF16)
        grads = (times_back(given, wo_ref[step]) * alive.astype(F32)).astype(BF16)
        for head in range(HEADS_STEP):
            cut = slice(head * HD, (head + 1) * HD)
            pair = jnp.concatenate([keys[:, cut], values[:, cut]], axis=1)
            qg_ref[head] = jnp.concatenate([queries[:, cut], grads[:, cut]], axis=1)
            first = step * dests + head * WAYS
            for half in range(WAYS):
                send_ref[first + half, :span, :] = pair
            for block in range(span // BLOCK):
                half = lax.rem(block + region, WAYS)
                to = span + (block // WAYS) * BLOCK
                send_ref[first + half, to : to + BLOCK, :] = qg_ref[head, block * BLOCK : (block + 1) * BLOCK, :]
        there = slice(step * dests, (step + 1) * dests)
        move = pltpu.make_async_copy(send_ref.at[there], send_hbm.at[there], out_sems.at[step])
        move.start()
        leaving.append(move)
    for move in leaving:
        move.wait()


def attend_kernel(
    region_ref,
    recv_ref,
    send_ref,
    kaug_ref,
    kv_ref,
    kt_ref,
    qg_ref,
    qa_ref,
    gm_ref,
    p_ref,
    wg_ref,
    top_ref,
    dkv_ref,
    dq_ref,
    koff_ref,
    qoff_ref,
):
    regions = recv_ref.shape[0]
    share = recv_ref.shape[1] // (WAYS + 1)
    span = share * WAYS
    me = region_ref[0]
    half = lax.rem(me, WAYS)
    busy = me < H * WAYS
    lane = lax.broadcasted_iota(jnp.int32, (BLOCK, 2 * HD), 1)
    row = lax.broadcasted_iota(jnp.int32, (BLOCK, 2 * HD), 0)
    low = (lax.broadcasted_iota(jnp.int32, (1, 2 * HD), 1) < HD).astype(BF16)
    high = (lax.broadcasted_iota(jnp.int32, (1, 2 * HD), 1) >= HD).astype(BF16)
    mark = (lax.broadcasted_iota(jnp.int32, (1, 2 * HD), 1) == HD).astype(BF16)
    lives = []
    for region in range(regions):
        there = recv_ref[region, :span, :].astype(F32)
        rows_live = jnp.sum((there == there).astype(F32)) * (1.0 / (2 * HD))
        lives.append(jnp.where(busy, jnp.clip(rows_live.astype(jnp.int32), 0, span), 0))
    key_total = query_total = jnp.int32(0)
    for region in range(regions):
        live = lives[region]
        koff_ref[region] = key_total
        qoff_ref[region] = query_total
        pair = recv_ref[region, :span, :]
        here = pl.ds(pl.multiple_of(key_total, BLOCK), span)
        kv_ref[here, :] = pair
        kaug_ref[here, :] = pair * low
        whole = lax.div(live, BLOCK)
        edge = pl.ds(pl.multiple_of(key_total + whole * BLOCK, BLOCK), BLOCK)
        good = row < live - whole * BLOCK
        bias = jnp.where(lane == HD, MASKED, 0.0)
        tail = kv_ref[edge, :].astype(F32)
        kv_ref[edge, :] = jnp.where(good, tail, 0.0).astype(BF16)
        kaug_ref[edge, :] = jnp.where(good, jnp.where(lane < HD, tail, 0.0), bias).astype(BF16)
        both = recv_ref[region, span : span + share, :]
        to = pl.ds(pl.multiple_of(query_total, BLOCK), share)
        qg_ref[to, :] = both
        qa_ref[to, :] = both * low + mark
        gm_ref[to, :] = both * high
        blocks = lax.div(live + BLOCK - 1, BLOCK)
        mine = lax.div(blocks + 1 - lax.rem(half + region, WAYS), WAYS)
        key_total += blocks * BLOCK
        query_total += mine * BLOCK
    rest = pl.ds(pl.multiple_of(key_total, BLOCK), KEY_STEP)
    none = jnp.zeros((KEY_STEP, 2 * HD), BF16)
    kv_ref[rest, :] = none
    kaug_ref[rest, :] = none + mark * MASKED
    rest = pl.ds(pl.multiple_of(query_total, BLOCK), QUERY_STEP)
    none = jnp.zeros((QUERY_STEP, 2 * HD), BF16)
    qg_ref[rest, :] = none
    qa_ref[rest, :] = none
    gm_ref[rest, :] = none
    key_steps = lax.div(key_total + KEY_STEP - 1, KEY_STEP)

    def turn(step, carry):
        keys = kaug_ref[pl.ds(pl.multiple_of(step * KEY_STEP, KEY_STEP), KEY_STEP), :]
        dkv_ref[pl.ds(pl.multiple_of(step * KEY_STEP, KEY_STEP), KEY_STEP), :] = jnp.zeros((KEY_STEP, 2 * HD), F32)
        kt_ref[step] = keys.astype(F32).T[:HD, :].astype(BF16)
        return carry

    lax.fori_loop(0, key_steps, turn, 0)

    def query_block(start, wide):
        at = pl.ds(pl.multiple_of(start, BLOCK), wide)

        def gather(step, state):
            top, total, dot = state
            here = pl.ds(pl.multiple_of(step * KEY_STEP, KEY_STEP), KEY_STEP)
            logits = times_back(kaug_ref[here, :], qa_ref[at, :]).reshape(KEY_STEP // 8, 8, wide)
            weight_grad = times_back(kv_ref[here, :], gm_ref[at, :]).reshape(KEY_STEP // 8, 8, wide)
            new_top = jnp.maximum(top, jnp.max(logits, axis=0))
            shrink = jnp.exp(top - new_top)
            raised = jnp.exp(logits - new_top[None])
            p_ref[step, :, :, :wide] = raised
            wg_ref[step, :, :, :wide] = weight_grad
            top_ref[step, :, :wide] = new_top
            total = total * shrink + jnp.sum(raised, axis=0)
            dot = dot * shrink + jnp.sum(raised * weight_grad, axis=0)
            return (new_top, total, dot)

        none = jnp.zeros((8, wide), F32)
        top, total, dot = lax.fori_loop(0, key_steps, gather, (none + MASKED, none, none))
        best = jnp.max(top, axis=0, keepdims=True)
        shrink = jnp.exp(top - best)
        whole = jnp.sum(total * shrink, axis=0, keepdims=True)
        inverse = 1.0 / whole
        delta = jnp.sum(dot * shrink, axis=0, keepdims=True) * inverse

        def spread(step, query_grad):
            here = pl.ds(pl.multiple_of(step * KEY_STEP, KEY_STEP), KEY_STEP)
            factor = jnp.exp(top_ref[step, :, :wide] - best) * inverse
            attention = p_ref[step, :, :, :wide] * factor[None]
            score_grad = attention * (wg_ref[step, :, :, :wide] - delta[None])
            attention = attention.reshape(KEY_STEP, wide).astype(BF16)
            score_grad = score_grad.reshape(KEY_STEP, wide).astype(BF16)
            both = qg_ref[at, :]
            lane = lax.broadcasted_iota(jnp.int32, (KEY_STEP, 2 * HD), 1)
            dkv_ref[here, :] += jnp.where(lane < HD, times(score_grad, both), times(attention, both))
            return query_grad + times(kt_ref[step], score_grad)

        query_grad = lax.fori_loop(0, key_steps, spread, jnp.zeros((HD, wide), F32))
        query_grad = query_grad * (1.0 / math.sqrt(HD))
        dq_ref[at, :] = jnp.concatenate([query_grad, query_grad], axis=0).T

    full = lax.div(query_total, QUERY_STEP)
    left = query_total - full * QUERY_STEP
    for index, wide in enumerate(QUERY_WIDTHS):
        above = QUERY_WIDTHS[index - 1] if index else 0

        @pl.when((left > above) & (left <= wide))
        def _(wide=wide):
            query_block(full * QUERY_STEP, wide)

    def whole_block(block, carry):
        query_block(block * QUERY_STEP, QUERY_STEP)
        return carry

    lax.fori_loop(0, full, whole_block, 0)

    lane = lax.broadcasted_iota(jnp.int32, (share // 2, 2 * HD), 1)
    for region in range(regions):
        here = pl.ds(pl.multiple_of(koff_ref[region], BLOCK), span)
        send_ref[region, :span, :] = dkv_ref[here, :].astype(BF16)
        first = dq_ref[pl.ds(pl.multiple_of(qoff_ref[region], BLOCK), share // 2), :]
        second = dq_ref[pl.ds(pl.multiple_of(qoff_ref[region] + share // 2, BLOCK), share // 2), :]
        send_ref[region, span:, :] = jnp.where(lane < HD, first, second).astype(BF16)


def return_kernel(
    region_ref, live_ref, recv_ref, taps_ref, wq_ref, wk_ref, wv_ref, out_ref, first_ref, last_ref,
    dk_ref, dv_ref, dq_ref, total_ref
):
    span, width = total_ref.shape[0] - 8, total_ref.shape[1]
    quarter = span // WAYS // 2
    region, live = region_ref[0], live_ref[0, 0]
    alive = lax.broadcasted_iota(jnp.int32, (span, 1), 0) < live
    for duo in range(HEADS_STEP // 2):
        cut = slice(duo * 2 * HD, (duo + 1) * 2 * HD)
        left, right = 2 * duo * WAYS, (2 * duo + 1) * WAYS
        first = recv_ref[left, :span, :].astype(F32) + recv_ref[left + 1, :span, :].astype(F32)
        second = recv_ref[right, :span, :].astype(F32) + recv_ref[right + 1, :span, :].astype(F32)
        key_grad = jnp.concatenate([first[:, :HD], second[:, :HD]], axis=1)
        value_grad = jnp.concatenate([first[:, HD:], second[:, HD:]], axis=1)
        dk_ref[:, cut] = jnp.where(alive, key_grad, 0.0).astype(BF16)
        dv_ref[:, cut] = jnp.where(alive, value_grad, 0.0).astype(BF16)
        for half in range(WAYS):
            shift = lax.rem(half + region, WAYS)
            one = recv_ref[left + half, span:, :].astype(F32)
            two = recv_ref[right + half, span:, :].astype(F32)
            low = jnp.concatenate([one[:, :HD], two[:, :HD]], axis=1)
            high = jnp.concatenate([one[:, HD:], two[:, HD:]], axis=1)
            for number, part in enumerate((low, high)):
                for piece in range(quarter // BLOCK):
                    index = number * (quarter // BLOCK) + piece
                    to = pl.multiple_of((WAYS * index + shift) * BLOCK, BLOCK)
                    dq_ref[pl.ds(to, BLOCK), cut] = part[piece * BLOCK : (piece + 1) * BLOCK, :]
    query_grad = jnp.where(alive, dq_ref[...], 0.0).astype(BF16)
    term = times_back(query_grad, wq_ref[...]) + (
        times_back(dk_ref[...], wk_ref[...]) + times_back(dv_ref[...], wv_ref[...])
    )
    step = pl.program_id(0)

    @pl.when(step == 0)
    def _():
        total_ref[:span, :] = term

    @pl.when(step > 0)
    def _():
        total_ref[:span, :] += term

    @pl.when(step == pl.num_programs(0) - 1)
    def _():
        total_ref[span:, :] = jnp.zeros((8, width), F32)
        input_grad = jnp.zeros((span, width), F32)
        for offset in range(KW):
            input_grad = input_grad + taps_ref[offset : offset + 1, :] * total_ref[offset : offset + span, :]
        out_ref[...] = input_grad.astype(BF16)
        last_ref[...] = input_grad[span - BLOCK :, :]
        first_ref[...] = total_ref[:8, :]


def finish_kernel(last_ref, later_ref, taps_ref, whole_ref, out_ref):
    del whole_ref
    rows, width = last_ref.shape
    total = last_ref[...]
    for offset in range(1, KW):
        reach = jnp.concatenate([jnp.zeros((rows - offset, width), F32), later_ref[:offset, :]], axis=0)
        total = total + taps_ref[offset : offset + 1, :] * reach
    out_ref[...] = total.astype(BF16)


def attend_call(region, gathered):
    regions, rows, _ = gathered.shape
    share = rows // (WAYS + 1)
    span = share * WAYS
    keys, queries = regions * span, regions * share
    key_steps = -(-keys // KEY_STEP)
    return pl.pallas_call(
        attend_kernel,
        name="attend",
        out_shape=jax.ShapeDtypeStruct((regions, span + share // 2, 2 * HD), BF16),
        in_specs=[smem(), vmem()],
        out_specs=vmem(),
        scratch_shapes=[
            pltpu.VMEM((keys + KEY_STEP, 2 * HD), BF16),
            pltpu.VMEM((keys + KEY_STEP, 2 * HD), BF16),
            pltpu.VMEM((key_steps, HD, KEY_STEP), BF16),
            pltpu.VMEM((queries + QUERY_STEP, 2 * HD), BF16),
            pltpu.VMEM((queries + QUERY_STEP, 2 * HD), BF16),
            pltpu.VMEM((queries + QUERY_STEP, 2 * HD), BF16),
            pltpu.VMEM((key_steps, KEY_STEP // 8, 8, QUERY_STEP), F32),
            pltpu.VMEM((key_steps, KEY_STEP // 8, 8, QUERY_STEP), F32),
            pltpu.VMEM((key_steps, 8, QUERY_STEP), F32),
            pltpu.VMEM((keys + KEY_STEP, 2 * HD), F32),
            pltpu.VMEM((queries + QUERY_STEP, 2 * HD), F32),
            pltpu.SMEM((regions,), jnp.int32),
            pltpu.SMEM((regions,), jnp.int32),
        ],
        compiler_params=params(50),
    )(region, gathered)


def shards(latents, output_grad, conv_kernel, w_query, w_key, w_value, w_out, live_counts):
    _, span, width = latents.shape
    regions = lax.axis_size("region")
    share = span // WAYS
    region = lax.axis_index("region").astype(jnp.int32).reshape(1)
    edge = passed_along(latents[:, span - (KW - 1) :, :], "tm", 1)
    steps = H // HEADS_STEP
    columns = HEADS_STEP * HD
    by_columns = pl.BlockSpec((width, columns), lambda i: (0, i))
    anywhere = pl.BlockSpec(memory_space=pl.ANY)
    sent = pl.pallas_call(
        project_kernel,
        name="project",
        out_shape=jax.ShapeDtypeStruct((regions, span + share, 2 * HD), BF16),
        in_specs=[smem(), smem()] + [anywhere] * 8,
        out_specs=anywhere,
        scratch_shapes=[
            pltpu.VMEM((span, width), BF16),
            pltpu.VMEM((KW - 1, width), BF16),
            pltpu.VMEM((span, width), BF16),
            pltpu.VMEM((KW, width), F32),
            pltpu.VMEM((steps, width, columns), BF16),
            pltpu.VMEM((steps, width, columns), BF16),
            pltpu.VMEM((steps, width, columns), BF16),
            pltpu.VMEM((steps, columns, width), BF16),
            pltpu.VMEM((H * WAYS, span + share, 2 * HD), BF16),
            pltpu.VMEM((HEADS_STEP, span, 2 * HD), BF16),
            pltpu.SemaphoreType.DMA((4 + 4 * steps,)),
            pltpu.SemaphoreType.DMA((steps,)),
        ],
        compiler_params=params(60),
    )(region, live_counts, latents[0], edge[0], output_grad[0], conv_kernel, w_query, w_key, w_value, w_out)
    gathered = lax.all_to_all(sent, "region", 0, 0, tiled=True)
    grads = attend_call(region, gathered)
    returned = lax.all_to_all(grads, "region", 0, 0, tiled=True)
    partial, first, last = pl.pallas_call(
        return_kernel,
        name="project_back",
        grid=(steps,),
        out_shape=(
            jax.ShapeDtypeStruct((span, width), BF16),
            jax.ShapeDtypeStruct((8, width), F32),
            jax.ShapeDtypeStruct((BLOCK, width), F32),
        ),
        in_specs=[
            smem(),
            smem(),
            pl.BlockSpec((HEADS_STEP * WAYS, span + share // 2, 2 * HD), lambda i: (i, 0, 0)),
            fixed(KW, width),
            by_columns,
            by_columns,
            by_columns,
        ],
        out_specs=(fixed(span, width), fixed(8, width), fixed(BLOCK, width)),
        scratch_shapes=[
            pltpu.VMEM((span, columns), BF16),
            pltpu.VMEM((span, columns), BF16),
            pltpu.VMEM((span, columns), F32),
            pltpu.VMEM((span + 8, width), F32),
        ],
        compiler_params=params(16),
    )(region, live_counts, returned, conv_kernel, w_query, w_key, w_value)
    later = passed_along(first, "tm", -1)
    input_grad = pl.pallas_call(
        finish_kernel,
        name="finish",
        grid=(1,),
        out_shape=jax.ShapeDtypeStruct((span, width), BF16),
        in_specs=[
            fixed(BLOCK, width),
            fixed(8, width),
            fixed(KW, width),
            pl.BlockSpec(memory_space=pl.ANY),
        ],
        out_specs=pl.BlockSpec((BLOCK, width), lambda i: (span // BLOCK - 1, 0)),
        input_output_aliases={3: 0},
        compiler_params=params(4),
    )(last, later, conv_kernel, partial)
    return input_grad[None]


def solution(mesh):
    in_specs = (
        P("region", "tm", None),
        P("region", "tm", None),
        P(),
        P(),
        P(),
        P(),
        P(),
        P("region", "tm"),
    )
    out_specs = P("region", "tm", None)
    return jax.shard_map(shards, mesh=mesh, in_specs=in_specs, out_specs=out_specs, check_vma=False)
```

```python
import math

import jax
import jax.numpy as jnp
from jax import lax
from jax.experimental import pallas as pl
from jax.experimental.pallas import tpu as pltpu
from jax.sharding import PartitionSpec as P

H = 12
HD = 64
KW = 4
WAYS = 2
BLOCK = 16
KEY_STEP = 512
QUERY_STEP = 1024
QUERY_WIDTHS = (512, 640, 768, 896, 1024)
MASKED = -1e30
HEADS_STEP = 4
BF16 = jnp.bfloat16
F32 = jnp.float32


def passed_along(block, axis, distance):
    devices = range(lax.axis_size(axis))
    route = [(i - distance, i) for i in devices if i - distance in devices]
    return lax.ppermute(block, axis, route)


def times(left, right):
    return lax.dot_general(left, right, (((1,), (0,)), ((), ())), preferred_element_type=F32)


def times_back(left, right):
    return lax.dot_general(left, right, (((1,), (1,)), ((), ())), preferred_element_type=F32)


def vmem():
    return pl.BlockSpec(memory_space=pltpu.VMEM)


def smem():
    return pl.BlockSpec(memory_space=pltpu.SMEM)


def fixed(*shape):
    return pl.BlockSpec(shape, lambda i: (0,) * len(shape))


def params(mebibytes):
    return pltpu.CompilerParams(vmem_limit_bytes=mebibytes * 1024 * 1024)


def grad_kernel(live_ref, grad_hbm, wo_hbm, out_ref, grad_ref, wo_ref, sems):
    moves = [
        pltpu.make_async_copy(grad_hbm, grad_ref, sems.at[0]),
        pltpu.make_async_copy(wo_hbm, wo_ref, sems.at[1]),
    ]
    for move in moves:
        move.start()
    for move in moves:
        move.wait()
    alive = lax.broadcasted_iota(jnp.int32, (out_ref.shape[0], 1), 0) < live_ref[0, 0]
    out_ref[...] = (times_back(grad_ref[...], wo_ref[...]) * alive.astype(F32)).astype(BF16)


def project_kernel(
    region_ref, live_ref, latents_hbm, edge_hbm, grads_hbm, taps_hbm, wq_hbm, wk_hbm, wv_hbm, send_hbm,
    latents_ref, edge_ref, grads_ref, taps_ref, wq_ref, wk_ref, wv_ref, send_ref, qg_ref, in_sems, out_sems
):
    span = latents_ref.shape[0]
    columns = HEADS_STEP * HD
    dests = HEADS_STEP * WAYS
    steps = H // HEADS_STEP
    region, live = region_ref[0], live_ref[0, 0]
    small = [
        pltpu.make_async_copy(source, target, in_sems.at[index])
        for index, (source, target) in enumerate(
            ((latents_hbm, latents_ref), (edge_hbm, edge_ref), (taps_hbm, taps_ref), (grads_hbm, grads_ref))
        )
    ]
    weights = []
    for step in range(steps):
        cut = slice(step * columns, (step + 1) * columns)
        parts = [(source.at[:, cut], target.at[step]) for source, target in ((wq_hbm, wq_ref), (wk_hbm, wk_ref), (wv_hbm, wv_ref))]
        weights.append(
            [pltpu.make_async_copy(*part, in_sems.at[4 + 3 * step + index]) for index, part in enumerate(parts)]
        )
    for move in small:
        move.start()
    for group in weights:
        for move in group:
            move.start()
    for move in small[:3]:
        move.wait()
    extended = jnp.concatenate([edge_ref[...].astype(F32), latents_ref[...].astype(F32)], axis=0)
    convolved = jnp.zeros(latents_ref.shape, F32)
    for offset in range(KW):
        start = KW - 1 - offset
        convolved = convolved + taps_ref[offset : offset + 1, :] * extended[start : start + span, :]
    hidden = convolved.astype(BF16)
    alive = lax.broadcasted_iota(jnp.int32, (span, 1), 0) < live
    small[3].wait()
    given = grads_ref[...]
    leaving = []
    for step in range(steps):
        for move in weights[step]:
            move.wait()
        queries = (times(hidden, wq_ref[step]).astype(BF16).astype(F32) * (1.0 / math.sqrt(HD))).astype(BF16)
        keys = jnp.where(alive, times(hidden, wk_ref[step]), jnp.nan).astype(BF16)
        values = jnp.where(alive, times(hidden, wv_ref[step]), jnp.nan).astype(BF16)
        grads = given[:, step * columns : (step + 1) * columns]
        for head in range(HEADS_STEP):
            cut = slice(head * HD, (head + 1) * HD)
            pair = jnp.concatenate([keys[:, cut], values[:, cut]], axis=1)
            qg_ref[head] = jnp.concatenate([queries[:, cut], grads[:, cut]], axis=1)
            first = step * dests + head * WAYS
            for half in range(WAYS):
                send_ref[first + half, :span, :] = pair
            for block in range(span // BLOCK):
                half = lax.rem(block + region, WAYS)
                to = span + (block // WAYS) * BLOCK
                send_ref[first + half, to : to + BLOCK, :] = qg_ref[head, block * BLOCK : (block + 1) * BLOCK, :]
        there = slice(step * dests, (step + 1) * dests)
        move = pltpu.make_async_copy(send_ref.at[there], send_hbm.at[there], out_sems.at[step])
        move.start()
        leaving.append(move)
    for move in leaving:
        move.wait()


def attend_kernel(
    region_ref,
    recv_ref,
    send_ref,
    kaug_ref,
    kv_ref,
    kt_ref,
    qg_ref,
    qa_ref,
    gm_ref,
    p_ref,
    wg_ref,
    top_ref,
    dkv_ref,
    dq_ref,
    koff_ref,
    qoff_ref,
):
    regions = recv_ref.shape[0]
    share = recv_ref.shape[1] // (WAYS + 1)
    span = share * WAYS
    me = region_ref[0]
    half = lax.rem(me, WAYS)
    busy = me < H * WAYS
    lane = lax.broadcasted_iota(jnp.int32, (BLOCK, 2 * HD), 1)
    row = lax.broadcasted_iota(jnp.int32, (BLOCK, 2 * HD), 0)
    low = (lax.broadcasted_iota(jnp.int32, (1, 2 * HD), 1) < HD).astype(BF16)
    high = (lax.broadcasted_iota(jnp.int32, (1, 2 * HD), 1) >= HD).astype(BF16)
    mark = (lax.broadcasted_iota(jnp.int32, (1, 2 * HD), 1) == HD).astype(BF16)
    lives = []
    for region in range(regions):
        there = recv_ref[region, :span, :].astype(F32)
        rows_live = jnp.sum((there == there).astype(F32)) * (1.0 / (2 * HD))
        lives.append(jnp.where(busy, jnp.clip(rows_live.astype(jnp.int32), 0, span), 0))
    key_total = query_total = jnp.int32(0)
    for region in range(regions):
        live = lives[region]
        koff_ref[region] = key_total
        qoff_ref[region] = query_total
        pair = recv_ref[region, :span, :]
        here = pl.ds(pl.multiple_of(key_total, BLOCK), span)
        kv_ref[here, :] = pair
        kaug_ref[here, :] = pair * low
        whole = lax.div(live, BLOCK)
        edge = pl.ds(pl.multiple_of(key_total + whole * BLOCK, BLOCK), BLOCK)
        good = row < live - whole * BLOCK
        bias = jnp.where(lane == HD, MASKED, 0.0)
        tail = kv_ref[edge, :].astype(F32)
        kv_ref[edge, :] = jnp.where(good, tail, 0.0).astype(BF16)
        kaug_ref[edge, :] = jnp.where(good, jnp.where(lane < HD, tail, 0.0), bias).astype(BF16)
        both = recv_ref[region, span : span + share, :]
        to = pl.ds(pl.multiple_of(query_total, BLOCK), share)
        qg_ref[to, :] = both
        qa_ref[to, :] = both * low + mark
        gm_ref[to, :] = both * high
        blocks = lax.div(live + BLOCK - 1, BLOCK)
        mine = lax.div(blocks + 1 - lax.rem(half + region, WAYS), WAYS)
        key_total += blocks * BLOCK
        query_total += mine * BLOCK
    rest = pl.ds(pl.multiple_of(key_total, BLOCK), KEY_STEP)
    none = jnp.zeros((KEY_STEP, 2 * HD), BF16)
    kv_ref[rest, :] = none
    kaug_ref[rest, :] = none + mark * MASKED
    rest = pl.ds(pl.multiple_of(query_total, BLOCK), QUERY_STEP)
    none = jnp.zeros((QUERY_STEP, 2 * HD), BF16)
    qg_ref[rest, :] = none
    qa_ref[rest, :] = none
    gm_ref[rest, :] = none
    key_steps = lax.div(key_total + KEY_STEP - 1, KEY_STEP)

    def turn(step, carry):
        keys = kaug_ref[pl.ds(pl.multiple_of(step * KEY_STEP, KEY_STEP), KEY_STEP), :]
        dkv_ref[pl.ds(pl.multiple_of(step * KEY_STEP, KEY_STEP), KEY_STEP), :] = jnp.zeros((KEY_STEP, 2 * HD), F32)
        kt_ref[step] = keys.astype(F32).T[:HD, :].astype(BF16)
        return carry

    lax.fori_loop(0, key_steps, turn, 0)

    def query_block(start, wide):
        at = pl.ds(pl.multiple_of(start, BLOCK), wide)

        def gather(step, state):
            top, total, dot = state
            here = pl.ds(pl.multiple_of(step * KEY_STEP, KEY_STEP), KEY_STEP)
            logits = times_back(kaug_ref[here, :], qa_ref[at, :]).reshape(KEY_STEP // 8, 8, wide)
            weight_grad = times_back(kv_ref[here, :], gm_ref[at, :]).reshape(KEY_STEP // 8, 8, wide)
            new_top = jnp.maximum(top, jnp.max(logits, axis=0))
            shrink = jnp.exp(top - new_top)
            raised = jnp.exp(logits - new_top[None])
            p_ref[step, :, :, :wide] = raised
            wg_ref[step, :, :, :wide] = weight_grad
            top_ref[step, :, :wide] = new_top
            total = total * shrink + jnp.sum(raised, axis=0)
            dot = dot * shrink + jnp.sum(raised * weight_grad, axis=0)
            return (new_top, total, dot)

        none = jnp.zeros((8, wide), F32)
        top, total, dot = lax.fori_loop(0, key_steps, gather, (none + MASKED, none, none))
        best = jnp.max(top, axis=0, keepdims=True)
        shrink = jnp.exp(top - best)
        whole = jnp.sum(total * shrink, axis=0, keepdims=True)
        inverse = 1.0 / whole
        delta = jnp.sum(dot * shrink, axis=0, keepdims=True) * inverse

        def spread(step, query_grad):
            here = pl.ds(pl.multiple_of(step * KEY_STEP, KEY_STEP), KEY_STEP)
            factor = jnp.exp(top_ref[step, :, :wide] - best) * inverse
            attention = p_ref[step, :, :, :wide] * factor[None]
            score_grad = attention * (wg_ref[step, :, :, :wide] - delta[None])
            attention = attention.reshape(KEY_STEP, wide).astype(BF16)
            score_grad = score_grad.reshape(KEY_STEP, wide).astype(BF16)
            both = qg_ref[at, :]
            lane = lax.broadcasted_iota(jnp.int32, (KEY_STEP, 2 * HD), 1)
            dkv_ref[here, :] += jnp.where(lane < HD, times(score_grad, both), times(attention, both))
            return query_grad + times(kt_ref[step], score_grad)

        query_grad = lax.fori_loop(0, key_steps, spread, jnp.zeros((HD, wide), F32))
        query_grad = query_grad * (1.0 / math.sqrt(HD))
        dq_ref[at, :] = jnp.concatenate([query_grad, query_grad], axis=0).T

    full = lax.div(query_total, QUERY_STEP)
    left = query_total - full * QUERY_STEP
    for index, wide in enumerate(QUERY_WIDTHS):
        above = QUERY_WIDTHS[index - 1] if index else 0

        @pl.when((left > above) & (left <= wide))
        def _(wide=wide):
            query_block(full * QUERY_STEP, wide)

    def whole_block(block, carry):
        query_block(block * QUERY_STEP, QUERY_STEP)
        return carry

    lax.fori_loop(0, full, whole_block, 0)

    lane = lax.broadcasted_iota(jnp.int32, (share // 2, 2 * HD), 1)
    for region in range(regions):
        here = pl.ds(pl.multiple_of(koff_ref[region], BLOCK), span)
        send_ref[region, :span, :] = dkv_ref[here, :].astype(BF16)
        first = dq_ref[pl.ds(pl.multiple_of(qoff_ref[region], BLOCK), share // 2), :]
        second = dq_ref[pl.ds(pl.multiple_of(qoff_ref[region] + share // 2, BLOCK), share // 2), :]
        send_ref[region, span:, :] = jnp.where(lane < HD, first, second).astype(BF16)


def return_kernel(
    region_ref, live_ref, recv_ref, taps_ref, wq_ref, wk_ref, wv_ref, out_ref, first_ref, last_ref,
    dk_ref, dv_ref, dq_ref, total_ref
):
    span, width = total_ref.shape[0] - 8, total_ref.shape[1]
    quarter = span // WAYS // 2
    region, live = region_ref[0], live_ref[0, 0]
    alive = lax.broadcasted_iota(jnp.int32, (span, 1), 0) < live
    for duo in range(H // 2):
        cut = slice(duo * 2 * HD, (duo + 1) * 2 * HD)
        left, right = 2 * duo * WAYS, (2 * duo + 1) * WAYS
        first = recv_ref[left, :span, :].astype(F32) + recv_ref[left + 1, :span, :].astype(F32)
        second = recv_ref[right, :span, :].astype(F32) + recv_ref[right + 1, :span, :].astype(F32)
        key_grad = jnp.concatenate([first[:, :HD], second[:, :HD]], axis=1)
        value_grad = jnp.concatenate([first[:, HD:], second[:, HD:]], axis=1)
        dk_ref[:, cut] = jnp.where(alive, key_grad, 0.0).astype(BF16)
        dv_ref[:, cut] = jnp.where(alive, value_grad, 0.0).astype(BF16)
        for half in range(WAYS):
            shift = lax.rem(half + region, WAYS)
            one = recv_ref[left + half, span:, :].astype(F32)
            two = recv_ref[right + half, span:, :].astype(F32)
            low = jnp.concatenate([one[:, :HD], two[:, :HD]], axis=1)
            high = jnp.concatenate([one[:, HD:], two[:, HD:]], axis=1)
            for number, part in enumerate((low, high)):
                for piece in range(quarter // BLOCK):
                    index = number * (quarter // BLOCK) + piece
                    to = pl.multiple_of((WAYS * index + shift) * BLOCK, BLOCK)
                    dq_ref[pl.ds(to, BLOCK), cut] = part[piece * BLOCK : (piece + 1) * BLOCK, :]
    query_grad = jnp.where(alive, dq_ref[...], 0.0).astype(BF16)
    total_ref[:span, :] = times_back(query_grad, wq_ref[...]) + (
        times_back(dk_ref[...], wk_ref[...]) + times_back(dv_ref[...], wv_ref[...])
    )
    total_ref[span:, :] = jnp.zeros((8, width), F32)
    first_ref[...] = total_ref[:8, :]
    input_grad = jnp.zeros((span, width), F32)
    for offset in range(KW):
        input_grad = input_grad + taps_ref[offset : offset + 1, :] * total_ref[offset : offset + span, :]
    out_ref[...] = input_grad.astype(BF16)
    last_ref[...] = input_grad[span - BLOCK :, :]


def finish_kernel(last_ref, later_ref, taps_ref, whole_ref, out_ref):
    del whole_ref
    rows, width = last_ref.shape
    total = last_ref[...]
    for offset in range(1, KW):
        reach = jnp.concatenate([jnp.zeros((rows - offset, width), F32), later_ref[:offset, :]], axis=0)
        total = total + taps_ref[offset : offset + 1, :] * reach
    out_ref[...] = total.astype(BF16)


def attend_call(region, gathered):
    regions, rows, _ = gathered.shape
    share = rows // (WAYS + 1)
    span = share * WAYS
    keys, queries = regions * span, regions * share
    key_steps = -(-keys // KEY_STEP)
    return pl.pallas_call(
        attend_kernel,
        name="attend",
        out_shape=jax.ShapeDtypeStruct((regions, span + share // 2, 2 * HD), BF16),
        in_specs=[smem(), vmem()],
        out_specs=vmem(),
        scratch_shapes=[
            pltpu.VMEM((keys + KEY_STEP, 2 * HD), BF16),
            pltpu.VMEM((keys + KEY_STEP, 2 * HD), BF16),
            pltpu.VMEM((key_steps, HD, KEY_STEP), BF16),
            pltpu.VMEM((queries + QUERY_STEP, 2 * HD), BF16),
            pltpu.VMEM((queries + QUERY_STEP, 2 * HD), BF16),
            pltpu.VMEM((queries + QUERY_STEP, 2 * HD), BF16),
            pltpu.VMEM((key_steps, KEY_STEP // 8, 8, QUERY_STEP), F32),
            pltpu.VMEM((key_steps, KEY_STEP // 8, 8, QUERY_STEP), F32),
            pltpu.VMEM((key_steps, 8, QUERY_STEP), F32),
            pltpu.VMEM((keys + KEY_STEP, 2 * HD), F32),
            pltpu.VMEM((queries + QUERY_STEP, 2 * HD), F32),
            pltpu.SMEM((regions,), jnp.int32),
            pltpu.SMEM((regions,), jnp.int32),
        ],
        compiler_params=params(50),
    )(region, gathered)


def shards(latents, output_grad, conv_kernel, w_query, w_key, w_value, w_out, live_counts):
    _, span, width = latents.shape
    regions = lax.axis_size("region")
    share = span // WAYS
    region = lax.axis_index("region").astype(jnp.int32).reshape(1)
    edge = passed_along(latents[:, span - (KW - 1) :, :], "tm", 1)
    steps = H // HEADS_STEP
    columns = HEADS_STEP * HD
    anywhere = pl.BlockSpec(memory_space=pl.ANY)
    grad_proj = pl.pallas_call(
        grad_kernel,
        name="project_grad",
        out_shape=jax.ShapeDtypeStruct((span, width), BF16),
        in_specs=[smem(), anywhere, anywhere],
        out_specs=vmem(),
        scratch_shapes=[
            pltpu.VMEM((span, width), BF16),
            pltpu.VMEM((width, width), BF16),
            pltpu.SemaphoreType.DMA((2,)),
        ],
        compiler_params=params(60),
        cost_estimate=pl.CostEstimate(
            flops=2 * span * width * width, bytes_accessed=2 * width * (width + 2 * span), transcendentals=0
        ),
    )(live_counts, output_grad[0], w_out)
    sent = pl.pallas_call(
        project_kernel,
        name="project",
        out_shape=jax.ShapeDtypeStruct((regions, span + share, 2 * HD), BF16),
        in_specs=[smem(), smem()] + [anywhere] * 7,
        out_specs=anywhere,
        scratch_shapes=[
            pltpu.VMEM((span, width), BF16),
            pltpu.VMEM((KW - 1, width), BF16),
            pltpu.VMEM((span, width), BF16),
            pltpu.VMEM((KW, width), F32),
            pltpu.VMEM((steps, width, columns), BF16),
            pltpu.VMEM((steps, width, columns), BF16),
            pltpu.VMEM((steps, width, columns), BF16),
            pltpu.VMEM((H * WAYS, span + share, 2 * HD), BF16),
            pltpu.VMEM((HEADS_STEP, span, 2 * HD), BF16),
            pltpu.SemaphoreType.DMA((4 + 3 * steps,)),
            pltpu.SemaphoreType.DMA((steps,)),
        ],
        compiler_params=params(54),
    )(region, live_counts, latents[0], edge[0], grad_proj, conv_kernel, w_query, w_key, w_value)
    gathered = lax.all_to_all(sent, "region", 0, 0, tiled=True)
    grads = attend_call(region, gathered)
    returned = lax.all_to_all(grads, "region", 0, 0, tiled=True)
    partial, first, last = pl.pallas_call(
        return_kernel,
        name="project_back",
        out_shape=(
            jax.ShapeDtypeStruct((span, width), BF16),
            jax.ShapeDtypeStruct((8, width), F32),
            jax.ShapeDtypeStruct((BLOCK, width), F32),
        ),
        in_specs=[smem(), smem()] + [vmem()] * 5,
        out_specs=[vmem()] * 3,
        scratch_shapes=[
            pltpu.VMEM((span, width), BF16),
            pltpu.VMEM((span, width), BF16),
            pltpu.VMEM((span, width), F32),
            pltpu.VMEM((span + 8, width), F32),
        ],
        compiler_params=params(16),
    )(region, live_counts, returned, conv_kernel, w_query, w_key, w_value)
    later = passed_along(first, "tm", -1)
    input_grad = pl.pallas_call(
        finish_kernel,
        name="finish",
        grid=(1,),
        out_shape=jax.ShapeDtypeStruct((span, width), BF16),
        in_specs=[
            fixed(BLOCK, width),
            fixed(8, width),
            fixed(KW, width),
            pl.BlockSpec(memory_space=pl.ANY),
        ],
        out_specs=pl.BlockSpec((BLOCK, width), lambda i: (span // BLOCK - 1, 0)),
        input_output_aliases={3: 0},
        compiler_params=params(4),
    )(last, later, conv_kernel, partial)
    return input_grad[None]


def solution(mesh):
    in_specs = (
        P("region", "tm", None),
        P("region", "tm", None),
        P(),
        P(),
        P(),
        P(),
        P(),
        P("region", "tm"),
    )
    out_specs = P("region", "tm", None)
    return jax.shard_map(shards, mesh=mesh, in_specs=in_specs, out_specs=out_specs, check_vma=False)
```

```python
import math

import jax
import jax.numpy as jnp
from jax import lax
from jax.experimental import pallas as pl
from jax.experimental.pallas import tpu as pltpu
from jax.sharding import PartitionSpec as P

H = 12
HD = 64
KW = 4
WAYS = 2
BLOCK = 16
KEY_STEP = 512
QUERY_STEP = 1024
QUERY_WIDTHS = (512, 640, 768, 896, 1024)
MASKED = -1e30
HEADS_STEP = 4
BF16 = jnp.bfloat16
F32 = jnp.float32


def passed_along(block, axis, distance):
    devices = range(lax.axis_size(axis))
    route = [(i - distance, i) for i in devices if i - distance in devices]
    return lax.ppermute(block, axis, route)


def times(left, right):
    return lax.dot_general(left, right, (((1,), (0,)), ((), ())), preferred_element_type=F32)


def times_back(left, right):
    return lax.dot_general(left, right, (((1,), (1,)), ((), ())), preferred_element_type=F32)


def vmem():
    return pl.BlockSpec(memory_space=pltpu.VMEM)


def smem():
    return pl.BlockSpec(memory_space=pltpu.SMEM)


def fixed(*shape):
    return pl.BlockSpec(shape, lambda i: (0,) * len(shape))


def params(mebibytes):
    return pltpu.CompilerParams(vmem_limit_bytes=mebibytes * 1024 * 1024)


def grad_kernel(live_ref, grad_hbm, wo_hbm, out_ref, grad_ref, wo_ref, sems):
    moves = [
        pltpu.make_async_copy(grad_hbm, grad_ref, sems.at[0]),
        pltpu.make_async_copy(wo_hbm, wo_ref, sems.at[1]),
    ]
    for move in moves:
        move.start()
    for move in moves:
        move.wait()
    alive = lax.broadcasted_iota(jnp.int32, (out_ref.shape[0], 1), 0) < live_ref[0, 0]
    out_ref[...] = (times_back(grad_ref[...], wo_ref[...]) * alive.astype(F32)).astype(BF16)


def project_kernel(
    region_ref, live_ref, latents_hbm, edge_ref, grads_hbm, taps_hbm, wq_hbm, wk_hbm, wv_hbm, send_hbm,
    latents_ref, grads_ref, taps_ref, wq_ref, wk_ref, wv_ref, send_ref, qg_ref, in_sems, out_sems
):
    span = latents_ref.shape[0]
    columns = HEADS_STEP * HD
    dests = HEADS_STEP * WAYS
    steps = H // HEADS_STEP
    region, live = region_ref[0], live_ref[0, 0]
    small = [
        pltpu.make_async_copy(source, target, in_sems.at[index])
        for index, (source, target) in enumerate(
            ((latents_hbm, latents_ref), (taps_hbm, taps_ref), (grads_hbm, grads_ref))
        )
    ]
    weights = []
    for step in range(steps):
        cut = slice(step * columns, (step + 1) * columns)
        parts = [(source.at[:, cut], target.at[step]) for source, target in ((wq_hbm, wq_ref), (wk_hbm, wk_ref), (wv_hbm, wv_ref))]
        weights.append(
            [pltpu.make_async_copy(*part, in_sems.at[3 + 3 * step + index]) for index, part in enumerate(parts)]
        )
    for move in small:
        move.start()
    for group in weights:
        for move in group:
            move.start()
    for move in small[:2]:
        move.wait()
    extended = jnp.concatenate([edge_ref[...].astype(F32), latents_ref[...].astype(F32)], axis=0)
    convolved = jnp.zeros(latents_ref.shape, F32)
    for offset in range(KW):
        start = KW - 1 - offset
        convolved = convolved + taps_ref[offset : offset + 1, :] * extended[start : start + span, :]
    hidden = convolved.astype(BF16)
    alive = lax.broadcasted_iota(jnp.int32, (span, 1), 0) < live
    small[2].wait()
    given = grads_ref[...]
    leaving = []
    for step in range(steps):
        for move in weights[step]:
            move.wait()
        queries = (times(hidden, wq_ref[step]).astype(BF16).astype(F32) * (1.0 / math.sqrt(HD))).astype(BF16)
        keys = jnp.where(alive, times(hidden, wk_ref[step]), jnp.nan).astype(BF16)
        values = jnp.where(alive, times(hidden, wv_ref[step]), jnp.nan).astype(BF16)
        grads = given[:, step * columns : (step + 1) * columns]
        for head in range(HEADS_STEP):
            cut = slice(head * HD, (head + 1) * HD)
            pair = jnp.concatenate([keys[:, cut], values[:, cut]], axis=1)
            qg_ref[head] = jnp.concatenate([queries[:, cut], grads[:, cut]], axis=1)
            first = step * dests + head * WAYS
            for half in range(WAYS):
                send_ref[first + half, :span, :] = pair
            for block in range(span // BLOCK):
                half = lax.rem(block + region, WAYS)
                to = span + (block // WAYS) * BLOCK
                send_ref[first + half, to : to + BLOCK, :] = qg_ref[head, block * BLOCK : (block + 1) * BLOCK, :]
        there = slice(step * dests, (step + 1) * dests)
        move = pltpu.make_async_copy(send_ref.at[there], send_hbm.at[there], out_sems.at[step])
        move.start()
        leaving.append(move)
    for move in leaving:
        move.wait()


def attend_kernel(
    region_ref,
    recv_ref,
    send_ref,
    kaug_ref,
    kv_ref,
    kt_ref,
    qg_ref,
    qa_ref,
    gm_ref,
    p_ref,
    wg_ref,
    top_ref,
    dkv_ref,
    dq_ref,
    koff_ref,
    qoff_ref,
):
    regions = recv_ref.shape[0]
    share = recv_ref.shape[1] // (WAYS + 1)
    span = share * WAYS
    me = region_ref[0]
    half = lax.rem(me, WAYS)
    busy = me < H * WAYS
    lane = lax.broadcasted_iota(jnp.int32, (BLOCK, 2 * HD), 1)
    row = lax.broadcasted_iota(jnp.int32, (BLOCK, 2 * HD), 0)
    low = (lax.broadcasted_iota(jnp.int32, (1, 2 * HD), 1) < HD).astype(BF16)
    high = (lax.broadcasted_iota(jnp.int32, (1, 2 * HD), 1) >= HD).astype(BF16)
    mark = (lax.broadcasted_iota(jnp.int32, (1, 2 * HD), 1) == HD).astype(BF16)
    lives = []
    for region in range(regions):
        there = recv_ref[region, :span, :].astype(F32)
        rows_live = jnp.sum((there == there).astype(F32)) * (1.0 / (2 * HD))
        lives.append(jnp.where(busy, jnp.clip(rows_live.astype(jnp.int32), 0, span), 0))
    key_total = query_total = jnp.int32(0)
    for region in range(regions):
        live = lives[region]
        koff_ref[region] = key_total
        qoff_ref[region] = query_total
        pair = recv_ref[region, :span, :]
        here = pl.ds(pl.multiple_of(key_total, BLOCK), span)
        kv_ref[here, :] = pair
        kaug_ref[here, :] = pair * low
        whole = lax.div(live, BLOCK)
        edge = pl.ds(pl.multiple_of(key_total + whole * BLOCK, BLOCK), BLOCK)
        good = row < live - whole * BLOCK
        bias = jnp.where(lane == HD, MASKED, 0.0)
        tail = kv_ref[edge, :].astype(F32)
        kv_ref[edge, :] = jnp.where(good, tail, 0.0).astype(BF16)
        kaug_ref[edge, :] = jnp.where(good, jnp.where(lane < HD, tail, 0.0), bias).astype(BF16)
        both = recv_ref[region, span : span + share, :]
        to = pl.ds(pl.multiple_of(query_total, BLOCK), share)
        qg_ref[to, :] = both
        qa_ref[to, :] = both * low + mark
        gm_ref[to, :] = both * high
        blocks = lax.div(live + BLOCK - 1, BLOCK)
        mine = lax.div(blocks + 1 - lax.rem(half + region, WAYS), WAYS)
        key_total += blocks * BLOCK
        query_total += mine * BLOCK
    rest = pl.ds(pl.multiple_of(key_total, BLOCK), KEY_STEP)
    none = jnp.zeros((KEY_STEP, 2 * HD), BF16)
    kv_ref[rest, :] = none
    kaug_ref[rest, :] = none + mark * MASKED
    rest = pl.ds(pl.multiple_of(query_total, BLOCK), QUERY_STEP)
    none = jnp.zeros((QUERY_STEP, 2 * HD), BF16)
    qg_ref[rest, :] = none
    qa_ref[rest, :] = none
    gm_ref[rest, :] = none
    key_steps = lax.div(key_total + KEY_STEP - 1, KEY_STEP)

    def turn(step, carry):
        keys = kaug_ref[pl.ds(pl.multiple_of(step * KEY_STEP, KEY_STEP), KEY_STEP), :]
        dkv_ref[pl.ds(pl.multiple_of(step * KEY_STEP, KEY_STEP), KEY_STEP), :] = jnp.zeros((KEY_STEP, 2 * HD), F32)
        kt_ref[step] = keys.astype(F32).T[:HD, :].astype(BF16)
        return carry

    lax.fori_loop(0, key_steps, turn, 0)

    def query_block(start, wide):
        at = pl.ds(pl.multiple_of(start, BLOCK), wide)

        def gather(step, state):
            top, total, dot = state
            here = pl.ds(pl.multiple_of(step * KEY_STEP, KEY_STEP), KEY_STEP)
            logits = times_back(kaug_ref[here, :], qa_ref[at, :]).reshape(KEY_STEP // 8, 8, wide)
            weight_grad = times_back(kv_ref[here, :], gm_ref[at, :]).reshape(KEY_STEP // 8, 8, wide)
            new_top = jnp.maximum(top, jnp.max(logits, axis=0))
            shrink = jnp.exp(top - new_top)
            raised = jnp.exp(logits - new_top[None])
            p_ref[step, :, :, :wide] = raised
            wg_ref[step, :, :, :wide] = weight_grad
            top_ref[step, :, :wide] = new_top
            total = total * shrink + jnp.sum(raised, axis=0)
            dot = dot * shrink + jnp.sum(raised * weight_grad, axis=0)
            return (new_top, total, dot)

        none = jnp.zeros((8, wide), F32)
        top, total, dot = lax.fori_loop(0, key_steps, gather, (none + MASKED, none, none))
        best = jnp.max(top, axis=0, keepdims=True)
        shrink = jnp.exp(top - best)
        whole = jnp.sum(total * shrink, axis=0, keepdims=True)
        inverse = 1.0 / whole
        delta = jnp.sum(dot * shrink, axis=0, keepdims=True) * inverse

        def spread(step, query_grad):
            here = pl.ds(pl.multiple_of(step * KEY_STEP, KEY_STEP), KEY_STEP)
            factor = jnp.exp(top_ref[step, :, :wide] - best) * inverse
            attention = p_ref[step, :, :, :wide] * factor[None]
            score_grad = attention * (wg_ref[step, :, :, :wide] - delta[None])
            attention = attention.reshape(KEY_STEP, wide).astype(BF16)
            score_grad = score_grad.reshape(KEY_STEP, wide).astype(BF16)
            both = qg_ref[at, :]
            lane = lax.broadcasted_iota(jnp.int32, (KEY_STEP, 2 * HD), 1)
            dkv_ref[here, :] += jnp.where(lane < HD, times(score_grad, both), times(attention, both))
            return query_grad + times(kt_ref[step], score_grad)

        query_grad = lax.fori_loop(0, key_steps, spread, jnp.zeros((HD, wide), F32))
        query_grad = query_grad * (1.0 / math.sqrt(HD))
        dq_ref[at, :] = jnp.concatenate([query_grad, query_grad], axis=0).T

    full = lax.div(query_total, QUERY_STEP)
    left = query_total - full * QUERY_STEP
    for index, wide in enumerate(QUERY_WIDTHS):
        above = QUERY_WIDTHS[index - 1] if index else 0

        @pl.when((left > above) & (left <= wide))
        def _(wide=wide):
            query_block(full * QUERY_STEP, wide)

    def whole_block(block, carry):
        query_block(block * QUERY_STEP, QUERY_STEP)
        return carry

    lax.fori_loop(0, full, whole_block, 0)

    lane = lax.broadcasted_iota(jnp.int32, (share // 2, 2 * HD), 1)
    for region in range(regions):
        here = pl.ds(pl.multiple_of(koff_ref[region], BLOCK), span)
        send_ref[region, :span, :] = dkv_ref[here, :].astype(BF16)
        first = dq_ref[pl.ds(pl.multiple_of(qoff_ref[region], BLOCK), share // 2), :]
        second = dq_ref[pl.ds(pl.multiple_of(qoff_ref[region] + share // 2, BLOCK), share // 2), :]
        send_ref[region, span:, :] = jnp.where(lane < HD, first, second).astype(BF16)


def return_kernel(
    region_ref, live_ref, recv_ref, taps_ref, wq_ref, wk_ref, wv_ref, out_ref, first_ref, last_ref,
    dk_ref, dv_ref, dq_ref, total_ref
):
    span, width = total_ref.shape[0] - 8, total_ref.shape[1]
    quarter = span // WAYS // 2
    region, live = region_ref[0], live_ref[0, 0]
    alive = lax.broadcasted_iota(jnp.int32, (span, 1), 0) < live
    for duo in range(H // 2):
        cut = slice(duo * 2 * HD, (duo + 1) * 2 * HD)
        left, right = 2 * duo * WAYS, (2 * duo + 1) * WAYS
        first = recv_ref[left, :span, :].astype(F32) + recv_ref[left + 1, :span, :].astype(F32)
        second = recv_ref[right, :span, :].astype(F32) + recv_ref[right + 1, :span, :].astype(F32)
        key_grad = jnp.concatenate([first[:, :HD], second[:, :HD]], axis=1)
        value_grad = jnp.concatenate([first[:, HD:], second[:, HD:]], axis=1)
        dk_ref[:, cut] = jnp.where(alive, key_grad, 0.0).astype(BF16)
        dv_ref[:, cut] = jnp.where(alive, value_grad, 0.0).astype(BF16)
        for half in range(WAYS):
            shift = lax.rem(half + region, WAYS)
            one = recv_ref[left + half, span:, :].astype(F32)
            two = recv_ref[right + half, span:, :].astype(F32)
            low = jnp.concatenate([one[:, :HD], two[:, :HD]], axis=1)
            high = jnp.concatenate([one[:, HD:], two[:, HD:]], axis=1)
            for number, part in enumerate((low, high)):
                for piece in range(quarter // BLOCK):
                    index = number * (quarter // BLOCK) + piece
                    to = pl.multiple_of((WAYS * index + shift) * BLOCK, BLOCK)
                    dq_ref[pl.ds(to, BLOCK), cut] = part[piece * BLOCK : (piece + 1) * BLOCK, :]
    query_grad = jnp.where(alive, dq_ref[...], 0.0).astype(BF16)
    total_ref[:span, :] = times_back(query_grad, wq_ref[...]) + (
        times_back(dk_ref[...], wk_ref[...]) + times_back(dv_ref[...], wv_ref[...])
    )
    total_ref[span:, :] = jnp.zeros((8, width), F32)
    first_ref[...] = total_ref[:8, :]
    input_grad = jnp.zeros((span, width), F32)
    for offset in range(KW):
        input_grad = input_grad + taps_ref[offset : offset + 1, :] * total_ref[offset : offset + span, :]
    out_ref[...] = input_grad.astype(BF16)
    last_ref[...] = input_grad[span - BLOCK :, :]


def finish_kernel(last_ref, later_ref, taps_ref, whole_ref, out_ref):
    del whole_ref
    rows, width = last_ref.shape
    total = last_ref[...]
    for offset in range(1, KW):
        reach = jnp.concatenate([jnp.zeros((rows - offset, width), F32), later_ref[:offset, :]], axis=0)
        total = total + taps_ref[offset : offset + 1, :] * reach
    out_ref[...] = total.astype(BF16)


def attend_call(region, gathered):
    regions, rows, _ = gathered.shape
    share = rows // (WAYS + 1)
    span = share * WAYS
    keys, queries = regions * span, regions * share
    key_steps = -(-keys // KEY_STEP)
    return pl.pallas_call(
        attend_kernel,
        name="attend",
        out_shape=jax.ShapeDtypeStruct((regions, span + share // 2, 2 * HD), BF16),
        in_specs=[smem(), vmem()],
        out_specs=vmem(),
        scratch_shapes=[
            pltpu.VMEM((keys + KEY_STEP, 2 * HD), BF16),
            pltpu.VMEM((keys + KEY_STEP, 2 * HD), BF16),
            pltpu.VMEM((key_steps, HD, KEY_STEP), BF16),
            pltpu.VMEM((queries + QUERY_STEP, 2 * HD), BF16),
            pltpu.VMEM((queries + QUERY_STEP, 2 * HD), BF16),
            pltpu.VMEM((queries + QUERY_STEP, 2 * HD), BF16),
            pltpu.VMEM((key_steps, KEY_STEP // 8, 8, QUERY_STEP), F32),
            pltpu.VMEM((key_steps, KEY_STEP // 8, 8, QUERY_STEP), F32),
            pltpu.VMEM((key_steps, 8, QUERY_STEP), F32),
            pltpu.VMEM((keys + KEY_STEP, 2 * HD), F32),
            pltpu.VMEM((queries + QUERY_STEP, 2 * HD), F32),
            pltpu.SMEM((regions,), jnp.int32),
            pltpu.SMEM((regions,), jnp.int32),
        ],
        compiler_params=params(50),
    )(region, gathered)


def shards(latents, output_grad, conv_kernel, w_query, w_key, w_value, w_out, live_counts):
    _, span, width = latents.shape
    regions = lax.axis_size("region")
    share = span // WAYS
    region = lax.axis_index("region").astype(jnp.int32).reshape(1)
    edge = passed_along(latents[:, span - (KW - 1) :, :], "tm", 1)
    steps = H // HEADS_STEP
    columns = HEADS_STEP * HD
    anywhere = pl.BlockSpec(memory_space=pl.ANY)
    grad_proj = pl.pallas_call(
        grad_kernel,
        name="project_grad",
        out_shape=jax.ShapeDtypeStruct((span, width), BF16),
        in_specs=[smem(), anywhere, anywhere],
        out_specs=vmem(),
        scratch_shapes=[
            pltpu.VMEM((span, width), BF16),
            pltpu.VMEM((width, width), BF16),
            pltpu.SemaphoreType.DMA((2,)),
        ],
        compiler_params=params(53),
        cost_estimate=pl.CostEstimate(
            flops=2 * span * width * width, bytes_accessed=2 * width * (width + 2 * span), transcendentals=0
        ),
    )(live_counts, output_grad[0], w_out)
    sent = pl.pallas_call(
        project_kernel,
        name="project",
        out_shape=jax.ShapeDtypeStruct((regions, span + share, 2 * HD), BF16),
        in_specs=[smem(), smem(), anywhere, vmem()] + [anywhere] * 5,
        out_specs=anywhere,
        scratch_shapes=[
            pltpu.VMEM((span, width), BF16),
            pltpu.VMEM((span, width), BF16),
            pltpu.VMEM((KW, width), F32),
            pltpu.VMEM((steps, width, columns), BF16),
            pltpu.VMEM((steps, width, columns), BF16),
            pltpu.VMEM((steps, width, columns), BF16),
            pltpu.VMEM((H * WAYS, span + share, 2 * HD), BF16),
            pltpu.VMEM((HEADS_STEP, span, 2 * HD), BF16),
            pltpu.SemaphoreType.DMA((3 + 3 * steps,)),
            pltpu.SemaphoreType.DMA((steps,)),
        ],
        compiler_params=params(53),
    )(region, live_counts, latents[0], edge[0], grad_proj, conv_kernel, w_query, w_key, w_value)
    gathered = lax.all_to_all(sent, "region", 0, 0, tiled=True)
    grads = attend_call(region, gathered)
    returned = lax.all_to_all(grads, "region", 0, 0, tiled=True)
    partial, first, last = pl.pallas_call(
        return_kernel,
        name="project_back",
        out_shape=(
            jax.ShapeDtypeStruct((span, width), BF16),
            jax.ShapeDtypeStruct((8, width), F32),
            jax.ShapeDtypeStruct((BLOCK, width), F32),
        ),
        in_specs=[smem(), smem()] + [vmem()] * 5,
        out_specs=[vmem()] * 3,
        scratch_shapes=[
            pltpu.VMEM((span, width), BF16),
            pltpu.VMEM((span, width), BF16),
            pltpu.VMEM((span, width), F32),
            pltpu.VMEM((span + 8, width), F32),
        ],
        compiler_params=params(16),
    )(region, live_counts, returned, conv_kernel, w_query, w_key, w_value)
    later = passed_along(first, "tm", -1)
    input_grad = pl.pallas_call(
        finish_kernel,
        name="finish",
        grid=(1,),
        out_shape=jax.ShapeDtypeStruct((span, width), BF16),
        in_specs=[
            fixed(BLOCK, width),
            fixed(8, width),
            fixed(KW, width),
            pl.BlockSpec(memory_space=pl.ANY),
        ],
        out_specs=pl.BlockSpec((BLOCK, width), lambda i: (span // BLOCK - 1, 0)),
        input_output_aliases={3: 0},
        compiler_params=params(4),
    )(last, later, conv_kernel, partial)
    return input_grad[None]


def solution(mesh):
    in_specs = (
        P("region", "tm", None),
        P("region", "tm", None),
        P(),
        P(),
        P(),
        P(),
        P(),
        P("region", "tm"),
    )
    out_specs = P("region", "tm", None)
    return jax.shard_map(shards, mesh=mesh, in_specs=in_specs, out_specs=out_specs, check_vma=False)
```

```python
import math

import jax
import jax.numpy as jnp
from jax import lax
from jax.experimental import pallas as pl
from jax.experimental.pallas import tpu as pltpu
from jax.sharding import PartitionSpec as P

H = 12
HD = 64
KW = 4
WAYS = 2
BLOCK = 16
KEY_STEP = 512
QUERY_STEP = 1024
QUERY_WIDTHS = (512, 640, 768, 896, 1024)
MASKED = -1e30
HEADS_STEP = 6
BF16 = jnp.bfloat16
F32 = jnp.float32


def passed_along(block, axis, distance):
    devices = range(lax.axis_size(axis))
    route = [(i - distance, i) for i in devices if i - distance in devices]
    return lax.ppermute(block, axis, route)


def times(left, right):
    return lax.dot_general(left, right, (((1,), (0,)), ((), ())), preferred_element_type=F32)


def times_back(left, right):
    return lax.dot_general(left, right, (((1,), (1,)), ((), ())), preferred_element_type=F32)


def vmem():
    return pl.BlockSpec(memory_space=pltpu.VMEM)


def smem():
    return pl.BlockSpec(memory_space=pltpu.SMEM)


def fixed(*shape):
    return pl.BlockSpec(shape, lambda i: (0,) * len(shape))


def params(mebibytes):
    return pltpu.CompilerParams(vmem_limit_bytes=mebibytes * 1024 * 1024)


def grad_kernel(live_ref, grad_hbm, wo_hbm, out_ref, grad_ref, wo_ref, sems):
    moves = [
        pltpu.make_async_copy(grad_hbm, grad_ref, sems.at[0]),
        pltpu.make_async_copy(wo_hbm, wo_ref, sems.at[1]),
    ]
    for move in moves:
        move.start()
    for move in moves:
        move.wait()
    alive = lax.broadcasted_iota(jnp.int32, (out_ref.shape[0], 1), 0) < live_ref[0, 0]
    out_ref[...] = (times_back(grad_ref[...], wo_ref[...]) * alive.astype(F32)).astype(BF16)


def project_kernel(
    region_ref, live_ref, latents_hbm, edge_ref, grads_hbm, taps_hbm, wq_hbm, wk_hbm, wv_hbm, send_hbm,
    latents_ref, grads_ref, taps_ref, wq_ref, wk_ref, wv_ref, send_ref, qg_ref, in_sems, out_sems
):
    span = latents_ref.shape[0]
    columns = HEADS_STEP * HD
    dests = HEADS_STEP * WAYS
    steps = H // HEADS_STEP
    region, live = region_ref[0], live_ref[0, 0]
    small = [
        pltpu.make_async_copy(source, target, in_sems.at[index])
        for index, (source, target) in enumerate(
            ((latents_hbm, latents_ref), (taps_hbm, taps_ref), (grads_hbm, grads_ref))
        )
    ]
    weights = []
    for step in range(steps):
        cut = slice(step * columns, (step + 1) * columns)
        parts = [(source.at[:, cut], target.at[step]) for source, target in ((wq_hbm, wq_ref), (wk_hbm, wk_ref), (wv_hbm, wv_ref))]
        weights.append(
            [pltpu.make_async_copy(*part, in_sems.at[3 + 3 * step + index]) for index, part in enumerate(parts)]
        )
    for move in small:
        move.start()
    for group in weights:
        for move in group:
            move.start()
    for move in small[:2]:
        move.wait()
    extended = jnp.concatenate([edge_ref[...].astype(F32), latents_ref[...].astype(F32)], axis=0)
    convolved = jnp.zeros(latents_ref.shape, F32)
    for offset in range(KW):
        start = KW - 1 - offset
        convolved = convolved + taps_ref[offset : offset + 1, :] * extended[start : start + span, :]
    hidden = convolved.astype(BF16)
    alive = lax.broadcasted_iota(jnp.int32, (span, 1), 0) < live
    small[2].wait()
    given = grads_ref[...]
    leaving = []
    for step in range(steps):
        for move in weights[step]:
            move.wait()
        queries = (times(hidden, wq_ref[step]).astype(BF16).astype(F32) * (1.0 / math.sqrt(HD))).astype(BF16)
        keys = jnp.where(alive, times(hidden, wk_ref[step]), jnp.nan).astype(BF16)
        values = jnp.where(alive, times(hidden, wv_ref[step]), jnp.nan).astype(BF16)
        grads = given[:, step * columns : (step + 1) * columns]
        for head in range(HEADS_STEP):
            cut = slice(head * HD, (head + 1) * HD)
            pair = jnp.concatenate([keys[:, cut], values[:, cut]], axis=1)
            qg_ref[head] = jnp.concatenate([queries[:, cut], grads[:, cut]], axis=1)
            first = step * dests + head * WAYS
            for half in range(WAYS):
                send_ref[first + half, :span, :] = pair
            for block in range(span // BLOCK):
                half = lax.rem(block + region, WAYS)
                to = span + (block // WAYS) * BLOCK
                send_ref[first + half, to : to + BLOCK, :] = qg_ref[head, block * BLOCK : (block + 1) * BLOCK, :]
        there = slice(step * dests, (step + 1) * dests)
        move = pltpu.make_async_copy(send_ref.at[there], send_hbm.at[there], out_sems.at[step])
        move.start()
        leaving.append(move)
    for move in leaving:
        move.wait()


def attend_kernel(
    region_ref,
    recv_ref,
    send_ref,
    kaug_ref,
    kv_ref,
    kt_ref,
    qg_ref,
    qa_ref,
    gm_ref,
    p_ref,
    wg_ref,
    top_ref,
    dkv_ref,
    dq_ref,
    koff_ref,
    qoff_ref,
):
    regions = recv_ref.shape[0]
    share = recv_ref.shape[1] // (WAYS + 1)
    span = share * WAYS
    me = region_ref[0]
    half = lax.rem(me, WAYS)
    busy = me < H * WAYS
    lane = lax.broadcasted_iota(jnp.int32, (BLOCK, 2 * HD), 1)
    row = lax.broadcasted_iota(jnp.int32, (BLOCK, 2 * HD), 0)
    low = (lax.broadcasted_iota(jnp.int32, (1, 2 * HD), 1) < HD).astype(BF16)
    high = (lax.broadcasted_iota(jnp.int32, (1, 2 * HD), 1) >= HD).astype(BF16)
    mark = (lax.broadcasted_iota(jnp.int32, (1, 2 * HD), 1) == HD).astype(BF16)
    lives = []
    for region in range(regions):
        there = recv_ref[region, :span, :].astype(F32)
        rows_live = jnp.sum((there == there).astype(F32)) * (1.0 / (2 * HD))
        lives.append(jnp.where(busy, jnp.clip(rows_live.astype(jnp.int32), 0, span), 0))
    key_total = query_total = jnp.int32(0)
    for region in range(regions):
        live = lives[region]
        koff_ref[region] = key_total
        qoff_ref[region] = query_total
        pair = recv_ref[region, :span, :]
        here = pl.ds(pl.multiple_of(key_total, BLOCK), span)
        kv_ref[here, :] = pair
        kaug_ref[here, :] = pair * low
        whole = lax.div(live, BLOCK)
        edge = pl.ds(pl.multiple_of(key_total + whole * BLOCK, BLOCK), BLOCK)
        good = row < live - whole * BLOCK
        bias = jnp.where(lane == HD, MASKED, 0.0)
        tail = kv_ref[edge, :].astype(F32)
        kv_ref[edge, :] = jnp.where(good, tail, 0.0).astype(BF16)
        kaug_ref[edge, :] = jnp.where(good, jnp.where(lane < HD, tail, 0.0), bias).astype(BF16)
        both = recv_ref[region, span : span + share, :]
        to = pl.ds(pl.multiple_of(query_total, BLOCK), share)
        qg_ref[to, :] = both
        qa_ref[to, :] = both * low + mark
        gm_ref[to, :] = both * high
        blocks = lax.div(live + BLOCK - 1, BLOCK)
        mine = lax.div(blocks + 1 - lax.rem(half + region, WAYS), WAYS)
        key_total += blocks * BLOCK
        query_total += mine * BLOCK
    rest = pl.ds(pl.multiple_of(key_total, BLOCK), KEY_STEP)
    none = jnp.zeros((KEY_STEP, 2 * HD), BF16)
    kv_ref[rest, :] = none
    kaug_ref[rest, :] = none + mark * MASKED
    rest = pl.ds(pl.multiple_of(query_total, BLOCK), QUERY_STEP)
    none = jnp.zeros((QUERY_STEP, 2 * HD), BF16)
    qg_ref[rest, :] = none
    qa_ref[rest, :] = none
    gm_ref[rest, :] = none
    key_steps = lax.div(key_total + KEY_STEP - 1, KEY_STEP)

    def turn(step, carry):
        keys = kaug_ref[pl.ds(pl.multiple_of(step * KEY_STEP, KEY_STEP), KEY_STEP), :]
        dkv_ref[pl.ds(pl.multiple_of(step * KEY_STEP, KEY_STEP), KEY_STEP), :] = jnp.zeros((KEY_STEP, 2 * HD), F32)
        kt_ref[step] = keys.astype(F32).T[:HD, :].astype(BF16)
        return carry

    lax.fori_loop(0, key_steps, turn, 0)

    def query_block(start, wide):
        at = pl.ds(pl.multiple_of(start, BLOCK), wide)

        def gather(step, state):
            top, total, dot = state
            here = pl.ds(pl.multiple_of(step * KEY_STEP, KEY_STEP), KEY_STEP)
            logits = times_back(kaug_ref[here, :], qa_ref[at, :]).reshape(KEY_STEP // 8, 8, wide)
            weight_grad = times_back(kv_ref[here, :], gm_ref[at, :]).reshape(KEY_STEP // 8, 8, wide)
            new_top = jnp.maximum(top, jnp.max(logits, axis=0))
            shrink = jnp.exp(top - new_top)
            raised = jnp.exp(logits - new_top[None])
            p_ref[step, :, :, :wide] = raised
            wg_ref[step, :, :, :wide] = weight_grad
            top_ref[step, :, :wide] = new_top
            total = total * shrink + jnp.sum(raised, axis=0)
            dot = dot * shrink + jnp.sum(raised * weight_grad, axis=0)
            return (new_top, total, dot)

        none = jnp.zeros((8, wide), F32)
        top, total, dot = lax.fori_loop(0, key_steps, gather, (none + MASKED, none, none))
        best = jnp.max(top, axis=0, keepdims=True)
        shrink = jnp.exp(top - best)
        whole = jnp.sum(total * shrink, axis=0, keepdims=True)
        inverse = 1.0 / whole
        delta = jnp.sum(dot * shrink, axis=0, keepdims=True) * inverse

        def spread(step, query_grad):
            here = pl.ds(pl.multiple_of(step * KEY_STEP, KEY_STEP), KEY_STEP)
            factor = jnp.exp(top_ref[step, :, :wide] - best) * inverse
            attention = p_ref[step, :, :, :wide] * factor[None]
            score_grad = attention * (wg_ref[step, :, :, :wide] - delta[None])
            attention = attention.reshape(KEY_STEP, wide).astype(BF16)
            score_grad = score_grad.reshape(KEY_STEP, wide).astype(BF16)
            both = qg_ref[at, :]
            lane = lax.broadcasted_iota(jnp.int32, (KEY_STEP, 2 * HD), 1)
            dkv_ref[here, :] += jnp.where(lane < HD, times(score_grad, both), times(attention, both))
            return query_grad + times(kt_ref[step], score_grad)

        query_grad = lax.fori_loop(0, key_steps, spread, jnp.zeros((HD, wide), F32))
        query_grad = query_grad * (1.0 / math.sqrt(HD))
        dq_ref[at, :] = jnp.concatenate([query_grad, query_grad], axis=0).T

    full = lax.div(query_total, QUERY_STEP)
    left = query_total - full * QUERY_STEP
    for index, wide in enumerate(QUERY_WIDTHS):
        above = QUERY_WIDTHS[index - 1] if index else 0

        @pl.when((left > above) & (left <= wide))
        def _(wide=wide):
            query_block(full * QUERY_STEP, wide)

    def whole_block(block, carry):
        query_block(block * QUERY_STEP, QUERY_STEP)
        return carry

    lax.fori_loop(0, full, whole_block, 0)

    lane = lax.broadcasted_iota(jnp.int32, (share // 2, 2 * HD), 1)
    for region in range(regions):
        here = pl.ds(pl.multiple_of(koff_ref[region], BLOCK), span)
        send_ref[region, :span, :] = dkv_ref[here, :].astype(BF16)
        first = dq_ref[pl.ds(pl.multiple_of(qoff_ref[region], BLOCK), share // 2), :]
        second = dq_ref[pl.ds(pl.multiple_of(qoff_ref[region] + share // 2, BLOCK), share // 2), :]
        send_ref[region, span:, :] = jnp.where(lane < HD, first, second).astype(BF16)


def return_kernel(
    region_ref, live_ref, recv_ref, taps_ref, wq_ref, wk_ref, wv_ref, out_ref, first_ref, last_ref,
    dk_ref, dv_ref, dq_ref, total_ref
):
    span, width = total_ref.shape[0] - 8, total_ref.shape[1]
    quarter = span // WAYS // 2
    region, live = region_ref[0], live_ref[0, 0]
    alive = lax.broadcasted_iota(jnp.int32, (span, 1), 0) < live
    for duo in range(H // 2):
        cut = slice(duo * 2 * HD, (duo + 1) * 2 * HD)
        left, right = 2 * duo * WAYS, (2 * duo + 1) * WAYS
        first = recv_ref[left, :span, :].astype(F32) + recv_ref[left + 1, :span, :].astype(F32)
        second = recv_ref[right, :span, :].astype(F32) + recv_ref[right + 1, :span, :].astype(F32)
        key_grad = jnp.concatenate([first[:, :HD], second[:, :HD]], axis=1)
        value_grad = jnp.concatenate([first[:, HD:], second[:, HD:]], axis=1)
        dk_ref[:, cut] = jnp.where(alive, key_grad, 0.0).astype(BF16)
        dv_ref[:, cut] = jnp.where(alive, value_grad, 0.0).astype(BF16)
        for half in range(WAYS):
            shift = lax.rem(half + region, WAYS)
            one = recv_ref[left + half, span:, :].astype(F32)
            two = recv_ref[right + half, span:, :].astype(F32)
            low = jnp.concatenate([one[:, :HD], two[:, :HD]], axis=1)
            high = jnp.concatenate([one[:, HD:], two[:, HD:]], axis=1)
            for number, part in enumerate((low, high)):
                for piece in range(quarter // BLOCK):
                    index = number * (quarter // BLOCK) + piece
                    to = pl.multiple_of((WAYS * index + shift) * BLOCK, BLOCK)
                    dq_ref[pl.ds(to, BLOCK), cut] = part[piece * BLOCK : (piece + 1) * BLOCK, :]
    query_grad = jnp.where(alive, dq_ref[...], 0.0).astype(BF16)
    total_ref[:span, :] = times_back(query_grad, wq_ref[...]) + (
        times_back(dk_ref[...], wk_ref[...]) + times_back(dv_ref[...], wv_ref[...])
    )
    total_ref[span:, :] = jnp.zeros((8, width), F32)
    first_ref[...] = total_ref[:8, :]
    input_grad = jnp.zeros((span, width), F32)
    for offset in range(KW):
        input_grad = input_grad + taps_ref[offset : offset + 1, :] * total_ref[offset : offset + span, :]
    out_ref[...] = input_grad.astype(BF16)
    last_ref[...] = input_grad[span - BLOCK :, :]


def finish_kernel(last_ref, later_ref, taps_ref, whole_ref, out_ref):
    del whole_ref
    rows, width = last_ref.shape
    total = last_ref[...]
    for offset in range(1, KW):
        reach = jnp.concatenate([jnp.zeros((rows - offset, width), F32), later_ref[:offset, :]], axis=0)
        total = total + taps_ref[offset : offset + 1, :] * reach
    out_ref[...] = total.astype(BF16)


def attend_call(region, gathered):
    regions, rows, _ = gathered.shape
    share = rows // (WAYS + 1)
    span = share * WAYS
    keys, queries = regions * span, regions * share
    key_steps = -(-keys // KEY_STEP)
    return pl.pallas_call(
        attend_kernel,
        name="attend",
        out_shape=jax.ShapeDtypeStruct((regions, span + share // 2, 2 * HD), BF16),
        in_specs=[smem(), vmem()],
        out_specs=vmem(),
        scratch_shapes=[
            pltpu.VMEM((keys + KEY_STEP, 2 * HD), BF16),
            pltpu.VMEM((keys + KEY_STEP, 2 * HD), BF16),
            pltpu.VMEM((key_steps, HD, KEY_STEP), BF16),
            pltpu.VMEM((queries + QUERY_STEP, 2 * HD), BF16),
            pltpu.VMEM((queries + QUERY_STEP, 2 * HD), BF16),
            pltpu.VMEM((queries + QUERY_STEP, 2 * HD), BF16),
            pltpu.VMEM((key_steps, KEY_STEP // 8, 8, QUERY_STEP), F32),
            pltpu.VMEM((key_steps, KEY_STEP // 8, 8, QUERY_STEP), F32),
            pltpu.VMEM((key_steps, 8, QUERY_STEP), F32),
            pltpu.VMEM((keys + KEY_STEP, 2 * HD), F32),
            pltpu.VMEM((queries + QUERY_STEP, 2 * HD), F32),
            pltpu.SMEM((regions,), jnp.int32),
            pltpu.SMEM((regions,), jnp.int32),
        ],
        compiler_params=params(50),
    )(region, gathered)


def shards(latents, output_grad, conv_kernel, w_query, w_key, w_value, w_out, live_counts):
    _, span, width = latents.shape
    regions = lax.axis_size("region")
    share = span // WAYS
    region = lax.axis_index("region").astype(jnp.int32).reshape(1)
    edge = passed_along(latents[:, span - (KW - 1) :, :], "tm", 1)
    steps = H // HEADS_STEP
    columns = HEADS_STEP * HD
    anywhere = pl.BlockSpec(memory_space=pl.ANY)
    grad_proj = pl.pallas_call(
        grad_kernel,
        name="project_grad",
        out_shape=jax.ShapeDtypeStruct((span, width), BF16),
        in_specs=[smem(), anywhere, anywhere],
        out_specs=vmem(),
        scratch_shapes=[
            pltpu.VMEM((span, width), BF16),
            pltpu.VMEM((width, width), BF16),
            pltpu.SemaphoreType.DMA((2,)),
        ],
        compiler_params=params(53),
        cost_estimate=pl.CostEstimate(
            flops=2 * span * width * width, bytes_accessed=2 * width * (width + 2 * span), transcendentals=0
        ),
    )(live_counts, output_grad[0], w_out)
    sent = pl.pallas_call(
        project_kernel,
        name="project",
        out_shape=jax.ShapeDtypeStruct((regions, span + share, 2 * HD), BF16),
        in_specs=[smem(), smem(), anywhere, vmem()] + [anywhere] * 5,
        out_specs=anywhere,
        scratch_shapes=[
            pltpu.VMEM((span, width), BF16),
            pltpu.VMEM((span, width), BF16),
            pltpu.VMEM((KW, width), F32),
            pltpu.VMEM((steps, width, columns), BF16),
            pltpu.VMEM((steps, width, columns), BF16),
            pltpu.VMEM((steps, width, columns), BF16),
            pltpu.VMEM((H * WAYS, span + share, 2 * HD), BF16),
            pltpu.VMEM((HEADS_STEP, span, 2 * HD), BF16),
            pltpu.SemaphoreType.DMA((3 + 3 * steps,)),
            pltpu.SemaphoreType.DMA((steps,)),
        ],
        compiler_params=params(53),
    )(region, live_counts, latents[0], edge[0], grad_proj, conv_kernel, w_query, w_key, w_value)
    gathered = lax.all_to_all(sent, "region", 0, 0, tiled=True)
    grads = attend_call(region, gathered)
    returned = lax.all_to_all(grads, "region", 0, 0, tiled=True)
    partial, first, last = pl.pallas_call(
        return_kernel,
        name="project_back",
        out_shape=(
            jax.ShapeDtypeStruct((span, width), BF16),
            jax.ShapeDtypeStruct((8, width), F32),
            jax.ShapeDtypeStruct((BLOCK, width), F32),
        ),
        in_specs=[smem(), smem()] + [vmem()] * 5,
        out_specs=[vmem()] * 3,
        scratch_shapes=[
            pltpu.VMEM((span, width), BF16),
            pltpu.VMEM((span, width), BF16),
            pltpu.VMEM((span, width), F32),
            pltpu.VMEM((span + 8, width), F32),
        ],
        compiler_params=params(16),
    )(region, live_counts, returned, conv_kernel, w_query, w_key, w_value)
    later = passed_along(first, "tm", -1)
    input_grad = pl.pallas_call(
        finish_kernel,
        name="finish",
        grid=(1,),
        out_shape=jax.ShapeDtypeStruct((span, width), BF16),
        in_specs=[
            fixed(BLOCK, width),
            fixed(8, width),
            fixed(KW, width),
            pl.BlockSpec(memory_space=pl.ANY),
        ],
        out_specs=pl.BlockSpec((BLOCK, width), lambda i: (span // BLOCK - 1, 0)),
        input_output_aliases={3: 0},
        compiler_params=params(4),
    )(last, later, conv_kernel, partial)
    return input_grad[None]


def solution(mesh):
    in_specs = (
        P("region", "tm", None),
        P("region", "tm", None),
        P(),
        P(),
        P(),
        P(),
        P(),
        P("region", "tm"),
    )
    out_specs = P("region", "tm", None)
    return jax.shard_map(shards, mesh=mesh, in_specs=in_specs, out_specs=out_specs, check_vma=False)
```

```python
import math

import jax
import jax.numpy as jnp
from jax import lax
from jax.experimental import pallas as pl
from jax.experimental.pallas import tpu as pltpu
from jax.sharding import PartitionSpec as P

H = 12
HD = 64
KW = 4
WAYS = 2
BLOCK = 16
KEY_STEP = 512
QUERY_STEP = 1024
QUERY_WIDTHS = (512, 640, 768, 896, 1024)
MASKED = -1e30
HEADS_STEP = 6
BF16 = jnp.bfloat16
F32 = jnp.float32


def passed_along(block, axis, distance):
    devices = range(lax.axis_size(axis))
    route = [(i - distance, i) for i in devices if i - distance in devices]
    return lax.ppermute(block, axis, route)


def times(left, right):
    return lax.dot_general(left, right, (((1,), (0,)), ((), ())), preferred_element_type=F32)


def times_back(left, right):
    return lax.dot_general(left, right, (((1,), (1,)), ((), ())), preferred_element_type=F32)


def vmem():
    return pl.BlockSpec(memory_space=pltpu.VMEM)


def smem():
    return pl.BlockSpec(memory_space=pltpu.SMEM)


def fixed(*shape):
    return pl.BlockSpec(shape, lambda i: (0,) * len(shape))


def params(mebibytes):
    return pltpu.CompilerParams(vmem_limit_bytes=mebibytes * 1024 * 1024)


def grad_kernel(live_ref, grad_hbm, wo_hbm, out_ref, grad_ref, wo_ref, sems):
    moves = [
        pltpu.make_async_copy(grad_hbm, grad_ref, sems.at[0]),
        pltpu.make_async_copy(wo_hbm, wo_ref, sems.at[1]),
    ]
    for move in moves:
        move.start()
    for move in moves:
        move.wait()
    alive = lax.broadcasted_iota(jnp.int32, (out_ref.shape[0], 1), 0) < live_ref[0, 0]
    out_ref[...] = (times_back(grad_ref[...], wo_ref[...]) * alive.astype(F32)).astype(BF16)


def project_kernel(
    region_ref, live_ref, latents_hbm, edge_ref, grads_hbm, taps_hbm, wq_hbm, wk_hbm, wv_hbm, send_hbm,
    latents_ref, grads_ref, taps_ref, wq_ref, wk_ref, wv_ref, send_ref, qg_ref, in_sems, out_sems
):
    span = latents_ref.shape[0]
    columns = HEADS_STEP * HD
    dests = HEADS_STEP * WAYS
    steps = H // HEADS_STEP
    region, live = region_ref[0], live_ref[0, 0]
    small = [
        pltpu.make_async_copy(source, target, in_sems.at[index])
        for index, (source, target) in enumerate(
            ((latents_hbm, latents_ref), (taps_hbm, taps_ref), (grads_hbm, grads_ref))
        )
    ]
    weights = []
    for step in range(steps):
        cut = slice(step * columns, (step + 1) * columns)
        parts = [(source.at[:, cut], target.at[step]) for source, target in ((wq_hbm, wq_ref), (wk_hbm, wk_ref), (wv_hbm, wv_ref))]
        weights.append(
            [pltpu.make_async_copy(*part, in_sems.at[3 + 3 * step + index]) for index, part in enumerate(parts)]
        )
    for move in small:
        move.start()
    for group in weights:
        for move in group:
            move.start()
    for move in small[:2]:
        move.wait()
    extended = jnp.concatenate([edge_ref[...].astype(F32), latents_ref[...].astype(F32)], axis=0)
    convolved = jnp.zeros(latents_ref.shape, F32)
    for offset in range(KW):
        start = KW - 1 - offset
        convolved = convolved + taps_ref[offset : offset + 1, :] * extended[start : start + span, :]
    hidden = convolved.astype(BF16)
    alive = lax.broadcasted_iota(jnp.int32, (span, 1), 0) < live
    small[2].wait()
    given = grads_ref[...]
    leaving = []
    for step in range(steps):
        weights[step][0].wait()
        queries = (times(hidden, wq_ref[step]).astype(BF16).astype(F32) * (1.0 / math.sqrt(HD))).astype(BF16)
        weights[step][1].wait()
        keys = jnp.where(alive, times(hidden, wk_ref[step]), jnp.nan).astype(BF16)
        weights[step][2].wait()
        values = jnp.where(alive, times(hidden, wv_ref[step]), jnp.nan).astype(BF16)
        grads = given[:, step * columns : (step + 1) * columns]
        for head in range(HEADS_STEP):
            cut = slice(head * HD, (head + 1) * HD)
            pair = jnp.concatenate([keys[:, cut], values[:, cut]], axis=1)
            qg_ref[head] = jnp.concatenate([queries[:, cut], grads[:, cut]], axis=1)
            first = step * dests + head * WAYS
            for half in range(WAYS):
                send_ref[first + half, :span, :] = pair
            for block in range(span // BLOCK):
                half = lax.rem(block + region, WAYS)
                to = span + (block // WAYS) * BLOCK
                send_ref[first + half, to : to + BLOCK, :] = qg_ref[head, block * BLOCK : (block + 1) * BLOCK, :]
        there = slice(step * dests, (step + 1) * dests)
        move = pltpu.make_async_copy(send_ref.at[there], send_hbm.at[there], out_sems.at[step])
        move.start()
        leaving.append(move)
    for move in leaving:
        move.wait()


def attend_kernel(
    region_ref,
    recv_ref,
    send_ref,
    kaug_ref,
    kv_ref,
    kt_ref,
    qg_ref,
    qa_ref,
    gm_ref,
    p_ref,
    wg_ref,
    top_ref,
    dkv_ref,
    dq_ref,
    koff_ref,
    qoff_ref,
):
    regions = recv_ref.shape[0]
    share = recv_ref.shape[1] // (WAYS + 1)
    span = share * WAYS
    me = region_ref[0]
    half = lax.rem(me, WAYS)
    busy = me < H * WAYS
    lane = lax.broadcasted_iota(jnp.int32, (BLOCK, 2 * HD), 1)
    row = lax.broadcasted_iota(jnp.int32, (BLOCK, 2 * HD), 0)
    low = (lax.broadcasted_iota(jnp.int32, (1, 2 * HD), 1) < HD).astype(BF16)
    high = (lax.broadcasted_iota(jnp.int32, (1, 2 * HD), 1) >= HD).astype(BF16)
    mark = (lax.broadcasted_iota(jnp.int32, (1, 2 * HD), 1) == HD).astype(BF16)
    lives = []
    for region in range(regions):
        there = recv_ref[region, :span, :].astype(F32)
        rows_live = jnp.sum((there == there).astype(F32)) * (1.0 / (2 * HD))
        lives.append(jnp.where(busy, jnp.clip(rows_live.astype(jnp.int32), 0, span), 0))
    key_total = query_total = jnp.int32(0)
    for region in range(regions):
        live = lives[region]
        koff_ref[region] = key_total
        qoff_ref[region] = query_total
        pair = recv_ref[region, :span, :]
        here = pl.ds(pl.multiple_of(key_total, BLOCK), span)
        kv_ref[here, :] = pair
        kaug_ref[here, :] = pair * low
        whole = lax.div(live, BLOCK)
        edge = pl.ds(pl.multiple_of(key_total + whole * BLOCK, BLOCK), BLOCK)
        good = row < live - whole * BLOCK
        bias = jnp.where(lane == HD, MASKED, 0.0)
        tail = kv_ref[edge, :].astype(F32)
        kv_ref[edge, :] = jnp.where(good, tail, 0.0).astype(BF16)
        kaug_ref[edge, :] = jnp.where(good, jnp.where(lane < HD, tail, 0.0), bias).astype(BF16)
        both = recv_ref[region, span : span + share, :]
        to = pl.ds(pl.multiple_of(query_total, BLOCK), share)
        qg_ref[to, :] = both
        qa_ref[to, :] = both * low + mark
        gm_ref[to, :] = both * high
        blocks = lax.div(live + BLOCK - 1, BLOCK)
        mine = lax.div(blocks + 1 - lax.rem(half + region, WAYS), WAYS)
        key_total += blocks * BLOCK
        query_total += mine * BLOCK
    rest = pl.ds(pl.multiple_of(key_total, BLOCK), KEY_STEP)
    none = jnp.zeros((KEY_STEP, 2 * HD), BF16)
    kv_ref[rest, :] = none
    kaug_ref[rest, :] = none + mark * MASKED
    rest = pl.ds(pl.multiple_of(query_total, BLOCK), QUERY_STEP)
    none = jnp.zeros((QUERY_STEP, 2 * HD), BF16)
    qg_ref[rest, :] = none
    qa_ref[rest, :] = none
    gm_ref[rest, :] = none
    key_steps = lax.div(key_total + KEY_STEP - 1, KEY_STEP)

    def turn(step, carry):
        keys = kaug_ref[pl.ds(pl.multiple_of(step * KEY_STEP, KEY_STEP), KEY_STEP), :]
        dkv_ref[pl.ds(pl.multiple_of(step * KEY_STEP, KEY_STEP), KEY_STEP), :] = jnp.zeros((KEY_STEP, 2 * HD), F32)
        kt_ref[step] = keys.astype(F32).T[:HD, :].astype(BF16)
        return carry

    lax.fori_loop(0, key_steps, turn, 0)

    def query_block(start, wide):
        at = pl.ds(pl.multiple_of(start, BLOCK), wide)

        def gather(step, state):
            top, total, dot = state
            here = pl.ds(pl.multiple_of(step * KEY_STEP, KEY_STEP), KEY_STEP)
            logits = times_back(kaug_ref[here, :], qa_ref[at, :]).reshape(KEY_STEP // 8, 8, wide)
            weight_grad = times_back(kv_ref[here, :], gm_ref[at, :]).reshape(KEY_STEP // 8, 8, wide)
            new_top = jnp.maximum(top, jnp.max(logits, axis=0))
            shrink = jnp.exp(top - new_top)
            raised = jnp.exp(logits - new_top[None])
            p_ref[step, :, :, :wide] = raised
            wg_ref[step, :, :, :wide] = weight_grad
            top_ref[step, :, :wide] = new_top
            total = total * shrink + jnp.sum(raised, axis=0)
            dot = dot * shrink + jnp.sum(raised * weight_grad, axis=0)
            return (new_top, total, dot)

        none = jnp.zeros((8, wide), F32)
        top, total, dot = lax.fori_loop(0, key_steps, gather, (none + MASKED, none, none))
        best = jnp.max(top, axis=0, keepdims=True)
        shrink = jnp.exp(top - best)
        whole = jnp.sum(total * shrink, axis=0, keepdims=True)
        inverse = 1.0 / whole
        delta = jnp.sum(dot * shrink, axis=0, keepdims=True) * inverse

        def spread(step, query_grad):
            here = pl.ds(pl.multiple_of(step * KEY_STEP, KEY_STEP), KEY_STEP)
            factor = jnp.exp(top_ref[step, :, :wide] - best) * inverse
            attention = p_ref[step, :, :, :wide] * factor[None]
            score_grad = attention * (wg_ref[step, :, :, :wide] - delta[None])
            attention = attention.reshape(KEY_STEP, wide).astype(BF16)
            score_grad = score_grad.reshape(KEY_STEP, wide).astype(BF16)
            both = qg_ref[at, :]
            lane = lax.broadcasted_iota(jnp.int32, (KEY_STEP, 2 * HD), 1)
            dkv_ref[here, :] += jnp.where(lane < HD, times(score_grad, both), times(attention, both))
            return query_grad + times(kt_ref[step], score_grad)

        query_grad = lax.fori_loop(0, key_steps, spread, jnp.zeros((HD, wide), F32))
        query_grad = query_grad * (1.0 / math.sqrt(HD))
        dq_ref[at, :] = jnp.concatenate([query_grad, query_grad], axis=0).T

    full = lax.div(query_total, QUERY_STEP)
    left = query_total - full * QUERY_STEP
    for index, wide in enumerate(QUERY_WIDTHS):
        above = QUERY_WIDTHS[index - 1] if index else 0

        @pl.when((left > above) & (left <= wide))
        def _(wide=wide):
            query_block(full * QUERY_STEP, wide)

    def whole_block(block, carry):
        query_block(block * QUERY_STEP, QUERY_STEP)
        return carry

    lax.fori_loop(0, full, whole_block, 0)

    lane = lax.broadcasted_iota(jnp.int32, (share // 2, 2 * HD), 1)
    for region in range(regions):
        here = pl.ds(pl.multiple_of(koff_ref[region], BLOCK), span)
        send_ref[region, :span, :] = dkv_ref[here, :].astype(BF16)
        first = dq_ref[pl.ds(pl.multiple_of(qoff_ref[region], BLOCK), share // 2), :]
        second = dq_ref[pl.ds(pl.multiple_of(qoff_ref[region] + share // 2, BLOCK), share // 2), :]
        send_ref[region, span:, :] = jnp.where(lane < HD, first, second).astype(BF16)


def return_kernel(
    region_ref, live_ref, recv_ref, taps_ref, wq_ref, wk_ref, wv_ref, out_ref, first_ref, last_ref,
    dk_ref, dv_ref, dq_ref, total_ref
):
    span, width = total_ref.shape[0] - 8, total_ref.shape[1]
    quarter = span // WAYS // 2
    region, live = region_ref[0], live_ref[0, 0]
    alive = lax.broadcasted_iota(jnp.int32, (span, 1), 0) < live
    for duo in range(H // 2):
        cut = slice(duo * 2 * HD, (duo + 1) * 2 * HD)
        left, right = 2 * duo * WAYS, (2 * duo + 1) * WAYS
        first = recv_ref[left, :span, :].astype(F32) + recv_ref[left + 1, :span, :].astype(F32)
        second = recv_ref[right, :span, :].astype(F32) + recv_ref[right + 1, :span, :].astype(F32)
        key_grad = jnp.concatenate([first[:, :HD], second[:, :HD]], axis=1)
        value_grad = jnp.concatenate([first[:, HD:], second[:, HD:]], axis=1)
        dk_ref[:, cut] = jnp.where(alive, key_grad, 0.0).astype(BF16)
        dv_ref[:, cut] = jnp.where(alive, value_grad, 0.0).astype(BF16)
        for half in range(WAYS):
            shift = lax.rem(half + region, WAYS)
            one = recv_ref[left + half, span:, :].astype(F32)
            two = recv_ref[right + half, span:, :].astype(F32)
            low = jnp.concatenate([one[:, :HD], two[:, :HD]], axis=1)
            high = jnp.concatenate([one[:, HD:], two[:, HD:]], axis=1)
            for number, part in enumerate((low, high)):
                for piece in range(quarter // BLOCK):
                    index = number * (quarter // BLOCK) + piece
                    to = pl.multiple_of((WAYS * index + shift) * BLOCK, BLOCK)
                    dq_ref[pl.ds(to, BLOCK), cut] = part[piece * BLOCK : (piece + 1) * BLOCK, :]
    query_grad = jnp.where(alive, dq_ref[...], 0.0).astype(BF16)
    total_ref[:span, :] = times_back(query_grad, wq_ref[...]) + (
        times_back(dk_ref[...], wk_ref[...]) + times_back(dv_ref[...], wv_ref[...])
    )
    total_ref[span:, :] = jnp.zeros((8, width), F32)
    first_ref[...] = total_ref[:8, :]
    input_grad = jnp.zeros((span, width), F32)
    for offset in range(KW):
        input_grad = input_grad + taps_ref[offset : offset + 1, :] * total_ref[offset : offset + span, :]
    out_ref[...] = input_grad.astype(BF16)
    last_ref[...] = input_grad[span - BLOCK :, :]


def finish_kernel(last_ref, later_ref, taps_ref, whole_ref, out_ref):
    del whole_ref
    rows, width = last_ref.shape
    total = last_ref[...]
    for offset in range(1, KW):
        reach = jnp.concatenate([jnp.zeros((rows - offset, width), F32), later_ref[:offset, :]], axis=0)
        total = total + taps_ref[offset : offset + 1, :] * reach
    out_ref[...] = total.astype(BF16)


def attend_call(region, gathered):
    regions, rows, _ = gathered.shape
    share = rows // (WAYS + 1)
    span = share * WAYS
    keys, queries = regions * span, regions * share
    key_steps = -(-keys // KEY_STEP)
    return pl.pallas_call(
        attend_kernel,
        name="attend",
        out_shape=jax.ShapeDtypeStruct((regions, span + share // 2, 2 * HD), BF16),
        in_specs=[smem(), vmem()],
        out_specs=vmem(),
        scratch_shapes=[
            pltpu.VMEM((keys + KEY_STEP, 2 * HD), BF16),
            pltpu.VMEM((keys + KEY_STEP, 2 * HD), BF16),
            pltpu.VMEM((key_steps, HD, KEY_STEP), BF16),
            pltpu.VMEM((queries + QUERY_STEP, 2 * HD), BF16),
            pltpu.VMEM((queries + QUERY_STEP, 2 * HD), BF16),
            pltpu.VMEM((queries + QUERY_STEP, 2 * HD), BF16),
            pltpu.VMEM((key_steps, KEY_STEP // 8, 8, QUERY_STEP), F32),
            pltpu.VMEM((key_steps, KEY_STEP // 8, 8, QUERY_STEP), F32),
            pltpu.VMEM((key_steps, 8, QUERY_STEP), F32),
            pltpu.VMEM((keys + KEY_STEP, 2 * HD), F32),
            pltpu.VMEM((queries + QUERY_STEP, 2 * HD), F32),
            pltpu.SMEM((regions,), jnp.int32),
            pltpu.SMEM((regions,), jnp.int32),
        ],
        compiler_params=params(50),
    )(region, gathered)


def shards(latents, output_grad, conv_kernel, w_query, w_key, w_value, w_out, live_counts):
    _, span, width = latents.shape
    regions = lax.axis_size("region")
    share = span // WAYS
    region = lax.axis_index("region").astype(jnp.int32).reshape(1)
    edge = passed_along(latents[:, span - (KW - 1) :, :], "tm", 1)
    steps = H // HEADS_STEP
    columns = HEADS_STEP * HD
    anywhere = pl.BlockSpec(memory_space=pl.ANY)
    grad_proj = pl.pallas_call(
        grad_kernel,
        name="project_grad",
        out_shape=jax.ShapeDtypeStruct((span, width), BF16),
        in_specs=[smem(), anywhere, anywhere],
        out_specs=vmem(),
        scratch_shapes=[
            pltpu.VMEM((span, width), BF16),
            pltpu.VMEM((width, width), BF16),
            pltpu.SemaphoreType.DMA((2,)),
        ],
        compiler_params=params(53),
        cost_estimate=pl.CostEstimate(
            flops=2 * span * width * width, bytes_accessed=2 * width * (width + 2 * span), transcendentals=0
        ),
    )(live_counts, output_grad[0], w_out)
    sent = pl.pallas_call(
        project_kernel,
        name="project",
        out_shape=jax.ShapeDtypeStruct((regions, span + share, 2 * HD), BF16),
        in_specs=[smem(), smem(), anywhere, vmem()] + [anywhere] * 5,
        out_specs=anywhere,
        scratch_shapes=[
            pltpu.VMEM((span, width), BF16),
            pltpu.VMEM((span, width), BF16),
            pltpu.VMEM((KW, width), F32),
            pltpu.VMEM((steps, width, columns), BF16),
            pltpu.VMEM((steps, width, columns), BF16),
            pltpu.VMEM((steps, width, columns), BF16),
            pltpu.VMEM((H * WAYS, span + share, 2 * HD), BF16),
            pltpu.VMEM((HEADS_STEP, span, 2 * HD), BF16),
            pltpu.SemaphoreType.DMA((3 + 3 * steps,)),
            pltpu.SemaphoreType.DMA((steps,)),
        ],
        compiler_params=params(53),
    )(region, live_counts, latents[0], edge[0], grad_proj, conv_kernel, w_query, w_key, w_value)
    gathered = lax.all_to_all(sent, "region", 0, 0, tiled=True)
    grads = attend_call(region, gathered)
    returned = lax.all_to_all(grads, "region", 0, 0, tiled=True)
    partial, first, last = pl.pallas_call(
        return_kernel,
        name="project_back",
        out_shape=(
            jax.ShapeDtypeStruct((span, width), BF16),
            jax.ShapeDtypeStruct((8, width), F32),
            jax.ShapeDtypeStruct((BLOCK, width), F32),
        ),
        in_specs=[smem(), smem()] + [vmem()] * 5,
        out_specs=[vmem()] * 3,
        scratch_shapes=[
            pltpu.VMEM((span, width), BF16),
            pltpu.VMEM((span, width), BF16),
            pltpu.VMEM((span, width), F32),
            pltpu.VMEM((span + 8, width), F32),
        ],
        compiler_params=params(16),
    )(region, live_counts, returned, conv_kernel, w_query, w_key, w_value)
    later = passed_along(first, "tm", -1)
    input_grad = pl.pallas_call(
        finish_kernel,
        name="finish",
        grid=(1,),
        out_shape=jax.ShapeDtypeStruct((span, width), BF16),
        in_specs=[
            fixed(BLOCK, width),
            fixed(8, width),
            fixed(KW, width),
            pl.BlockSpec(memory_space=pl.ANY),
        ],
        out_specs=pl.BlockSpec((BLOCK, width), lambda i: (span // BLOCK - 1, 0)),
        input_output_aliases={3: 0},
        compiler_params=params(4),
    )(last, later, conv_kernel, partial)
    return input_grad[None]


def solution(mesh):
    in_specs = (
        P("region", "tm", None),
        P("region", "tm", None),
        P(),
        P(),
        P(),
        P(),
        P(),
        P("region", "tm"),
    )
    out_specs = P("region", "tm", None)
    return jax.shard_map(shards, mesh=mesh, in_specs=in_specs, out_specs=out_specs, check_vma=False)
```
